32 devices in a mesh: sub: 2 (over core), row: 4 (over y, x), col: 4 (over z).
Axes of the slice: x: 2, y: 2, z: 4, core: 2. Of those that a mesh axis runs over, the one named last changes fastest.
Arguments:
- front: float32 [16, 8, 128, 32, 4, 128], P(None, ('sub', 'row'), None, None, 'col'), may hold values from -2.4 to 7.5, as said below
- child_tiles: bfloat16 [4096, 128, 128], P(('sub', 'row', 'col')), may hold values from -2.390625 to 2.390625
- tile_owner: int32 [4096, 1], P(('sub', 'row', 'col')), may hold values from 0 to 31; in each aligned block of 128 rows (0 to 127, 128 to 255, ...) at most 8 rows name the same one
- tile_slot: int32 [4096], P(('sub', 'row', 'col')), may hold values from 2 to 511
Outputs:
- updated: float32 [16, 8, 128, 32, 4, 128], P(None, ('sub', 'row'), None, None, 'col')
- panel: bfloat16 [16, 8, 128, 2, 4, 128], P(None, ('sub', 'row'), None, None, 'col')
The draws below stay inside these ranges and needn't reach their ends.
Inputs may be any that keep to these rules, and one draw needn't show every extreme that they name: The leading 1024 x 1024 block of front, made symmetric from its lower triangle, is positive definite. `tile_owner`: at most 8 of the tiles of one device go to one owner.
All inputs are finite; a program needn't handle non-finite values.
Results may differ from the reference program's by a relative error of at most 0.0038.
Values may be sent and summed in bfloat16 or wider, within the bound.
No kernel may reach another device: no remote copies, remote signals or barrier semaphores. Data moves between devices by JAX's collectives and lax.ppermute only.
A program may use at most 256 MiB of HBM per device.

```python
import math
import jax
import jax.numpy as jnp
import numpy as np
from jax import lax

P_SIZE = 16384
NB = 1024
TB = 128
TILES_DEV = 128
CAP = 8
TILES = 4096
ROW_TILES = 16
COL_TILES = 32
N_SUB = 2
N_ROW = 4
N_COL = 4
DEVICES = 32


def draw_front(key, part):
    group_count = N_SUB * N_ROW
    row_tiles = P_SIZE // TB // group_count
    col_tiles = P_SIZE // TB // N_COL
    extent = (row_tiles, group_count, TB, col_tiles, N_COL, TB)
    key_base, key_mix, key_diag = jax.random.split(key, 3)
    base = jnp.clip(0.4 * jax.random.normal(key_base, extent, jnp.float32), -2.4, 2.4)
    mixing = jnp.clip(jax.random.normal(key_mix, (NB, NB), jnp.float32), -4.0, 4.0)
    lengths = jnp.sqrt(jnp.sum(mixing * mixing, 1, keepdims=True) + 1e-06)
    unit_rows = mixing / lengths
    gram = jnp.dot(unit_rows, unit_rows.T, precision=lax.Precision.HIGHEST, preferred_element_type=jnp.float32)
    shift = jax.random.uniform(key_diag, (NB,), jnp.float32, 2.5, 3.5)
    identity = jnp.eye(NB, dtype=jnp.bool_)
    pivot = jnp.where(identity, 4.0 + shift[:, None], 4.0 * gram)
    pivot_tiles = pivot.reshape(NB // TB, TB, NB // (TB * N_COL), N_COL, TB)
    return base.at[0, :NB // TB, :, :NB // (TB * N_COL), :, :].set(pivot_tiles)


def touch_ends(array, own_key, low, largest):
    shape = array.shape
    place = [jax.random.randint(jax.random.fold_in(own_key, axis), (), 0, shape[axis]) for axis in range(len(shape))]
    array = array.at[tuple(place)].set(low)
    longest = shape.index(max(shape))
    place[longest] = (place[longest] + 1) % shape[longest]
    return array.at[tuple(place)].set(largest)


def levels(key, shape, cuts, low, largest):
    factor_of = 1.0
    for position, shards_of in cuts:
        steps = jax.random.uniform(jax.random.fold_in(jax.random.fold_in(key, 6), position), (shards_of,), jnp.float32, low / len(cuts), largest / len(cuts))
        factor_of = factor_of * jnp.repeat(jnp.exp(steps), shape[position] // shards_of).reshape((-1,) + (1,) * (len(shape) - 1 - position))
    return factor_of


def routed_block(own_key, own, number, rows, count, top, limit, slope):
    sequence = jax.random.permutation(own_key, count)
    heavy_load, common = load_shares(count, rows * top, limit, slope, True), load_shares(count, rows * top, limit, slope, False)
    places = jnp.arange(count)

    def named(sizes, offset_by):
        used = int((sizes > 0).sum())
        fixed = max(1, used // 4)
        shifted = fixed + (places - fixed + offset_by * (used - fixed)) % max(1, count - fixed)
        return jnp.zeros((count,), jnp.int32).at[sequence[jnp.where(places < fixed, places, shifted)]].set(jnp.asarray(sizes, jnp.int32))

    sizes = jnp.where(number % 4 == 0, named(heavy_load, number // 4), named(common, number - number // 4 - 1))
    mixed = jax.random.permutation(jax.random.fold_in(own, 3), count)
    giver, taker = mixed[0:count // 2 * 2:2], mixed[1:count // 2 * 2:2]
    margin = jnp.minimum(sizes[giver] - 1, limit - sizes[taker]) // 2
    margin = jnp.where((giver == sequence[0]) | (taker == sequence[0]) | (sizes[taker] == 0), 0, jnp.maximum(margin, 0))
    shifted = jax.random.randint(jax.random.fold_in(own, 4), (count // 2,), 0, 1 << 20) % (margin + 1)
    sizes = sizes.at[giver].add(-shifted).at[taker].add(shifted)
    labels = jnp.searchsorted(jnp.cumsum(sizes), jnp.arange(rows * top), side="right").astype(jnp.int32)
    table = labels.reshape(top, rows).T
    table = table[jax.random.permutation(jax.random.fold_in(own, 1), rows)]
    offset_by = jax.random.randint(jax.random.fold_in(own, 2), (rows, 1), 0, top)
    return jnp.take_along_axis(table, (jnp.arange(top)[None, :] + offset_by) % top, axis=1)


def load_shares(count, total, most, lean, full):
    loads = [(1 << 20) // math.isqrt(rank ** lean) + 1 for rank in range(1, count + 1)]
    largest = most if full else min(most, max(-(-total // count), total * loads[0] // sum(loads)))
    least = 1 if total - largest >= count - 1 else 0
    counts, spare = [largest] + [least] * (count - 1), total - largest - least * (count - 1)
    while spare > 0:
        movable = [i for i in range(1, count) if counts[i] < largest] or [i for i in range(1, count) if counts[i] < most]
        whole, budget = sum([loads[i] for i in movable]), spare
        for i in movable:
            extra = min(most - counts[i], max(1, budget * loads[i] // whole), spare)
            counts[i] = counts[i] + extra
            spare = spare - extra
    return np.array(counts)


def noise(own_key, shape, deviation, limit, cuts=(), held_as=jnp.bfloat16):
    drawn = jax.random.normal(own_key, shape, jnp.float32) * deviation
    if len(cuts) > 0:
        drawn = levels(own_key, shape, cuts, -0.22, 0.18) * drawn
    return jnp.clip(drawn, min=-limit, max=limit).astype(held_as)


def setup_inputs(seed: int = 0) -> dict:
    key_list = jax.random.split(jax.random.key(seed), 5)
    front = draw_front(jax.random.fold_in(key_list[4], 71), 0)
    child_tiles = noise(key_list[1], (TILES, TB, TB), 0.4, 2.390625, ((0, 32),))
    tile_owner_keys = jax.random.split(jax.random.fold_in(key_list[2], 1), TILES // TILES_DEV)
    tile_owner_turns = jax.random.permutation(jax.random.fold_in(key_list[2], 3), TILES // TILES_DEV)
    tile_owner = jax.vmap(lambda own, number: routed_block(jax.random.fold_in(key_list[2], 2), own, number, TILES_DEV, DEVICES, 1, CAP, 2))(tile_owner_keys, tile_owner_turns).reshape((TILES, 1))
    tile_slot = touch_ends(jax.random.randint(key_list[3], (TILES,), NB // (TB * N_COL), ROW_TILES * COL_TILES), jax.random.fold_in(key_list[3], 1), NB // (TB * N_COL), (ROW_TILES * COL_TILES) - 1).astype(jnp.int32)
    return dict(front=front, child_tiles=child_tiles, tile_owner=tile_owner, tile_slot=tile_slot)


def reference(front, child_tiles, tile_owner, tile_slot):
    group_count = N_SUB * N_ROW
    tile_total = P_SIZE // TB
    col_tiles = tile_total // N_COL
    owners = tile_owner[:, 0]
    tile_row = tile_slot // col_tiles * group_count + owners // N_COL
    tile_col = tile_slot % col_tiles * N_COL + owners % N_COL
    tiled = front.reshape(tile_total, TB, tile_total, TB)
    tiled = tiled.at[tile_row, :, tile_col, :].add(child_tiles.astype(jnp.float32))
    assembled = tiled.reshape(P_SIZE, P_SIZE)
    pivot = assembled[:NB, :NB]
    symmetric = jnp.tril(pivot) + jnp.tril(pivot, -1).T
    factor = jnp.linalg.cholesky(symmetric)
    below = jax.scipy.linalg.solve_triangular(factor, assembled[NB:, :NB].T, lower=True).T
    panel = jnp.concatenate([factor, below], 0).astype(jnp.bfloat16)
    lower = panel[NB:].astype(jnp.float32)
    trailing = assembled[NB:, NB:] - jnp.dot(lower.astype(jnp.float32), lower.T.astype(jnp.float32), precision=lax.Precision.HIGHEST, preferred_element_type=jnp.float32)
    updated = assembled.at[NB:, NB:].set(trailing)
    panel_out = panel.reshape(tile_total // group_count, group_count, TB, NB // (TB * N_COL), N_COL, TB)
    return (updated.reshape(front.shape), panel_out)
```

```python
import functools

import jax
import jax.numpy as jnp
from jax import lax
from jax.experimental import pallas as pl
from jax.experimental.pallas import tpu as pltpu
from jax.sharding import PartitionSpec as P

NB = 1024
ANY = pl.ANY
EXACT = lax.Precision.HIGHEST
VMEM_LIMIT = 56 * 1024 * 1024


def params():
    return pltpu.CompilerParams(vmem_limit_bytes=VMEM_LIMIT)


def contract(a, b, dim_a, dim_b):
    return lax.dot_general(
        a, b, (((dim_a,), (dim_b,)), ((), ())), precision=EXACT, preferred_element_type=jnp.float32
    )


def pack_kernel(owner, slot, tiles, outgoing, targets, counts, sem, *, capacity):
    tile_count = tiles.shape[0]
    dev_count = counts.shape[0]

    def clear(d, _):
        counts[d] = 0
        for r in range(capacity):
            targets[d * capacity + r] = -1
        return 0

    lax.fori_loop(0, dev_count, clear, 0)

    def send(k, _):
        d = owner[k]
        place = d * capacity + counts[d]
        counts[d] = counts[d] + 1
        targets[place] = slot[k]
        pltpu.make_async_copy(tiles.at[k], outgoing.at[place], sem).start()
        return 0

    lax.fori_loop(0, tile_count, send, 0)
    pltpu.make_async_copy(tiles, outgoing.at[pl.ds(0, tile_count)], sem).wait()


def pack(owner, slot, tiles, dev_count, capacity):
    smem = pl.BlockSpec(memory_space=pltpu.SMEM)
    return pl.pallas_call(
        functools.partial(pack_kernel, capacity=capacity),
        in_specs=[smem, smem, pl.BlockSpec(memory_space=ANY)],
        out_specs=[pl.BlockSpec(memory_space=ANY), smem],
        out_shape=[
            jax.ShapeDtypeStruct((dev_count * capacity,) + tiles.shape[1:], tiles.dtype),
            jax.ShapeDtypeStruct((dev_count * capacity,), jnp.int32),
        ],
        scratch_shapes=[pltpu.SMEM((dev_count,), jnp.int32), pltpu.SemaphoreType.DMA],
        compiler_params=params(),
        cost_estimate=pl.CostEstimate(flops=0, bytes_accessed=2 * tiles.size * 2, transcendentals=0),
        name="pack_children",
    )(owner, slot, tiles)


def eliminate(tile):
    n = tile.shape[0]
    groups = n // 8
    rows = lax.broadcasted_iota(jnp.int32, (8, n), 0)
    lanes = lax.broadcasted_iota(jnp.int32, (8, n), 1)
    upper = [tile[8 * h : 8 * h + 8, :] for h in range(groups)]
    ops = [jnp.where(lanes == rows + 8 * h, 1.0, 0.0).astype(jnp.float32) for h in range(groups)]
    column = [jnp.broadcast_to(upper[h][:, 0:1], (8, n)) for h in range(groups)]
    for j in range(n):
        g, u = divmod(j, 8)
        inverse = 1.0 / column[g][u : u + 1, :]
        row = upper[g][u : u + 1, :] * inverse
        row_ops = ops[g][u : u + 1, :] * inverse
        ahead = [None] * groups
        if j + 1 < n:
            g1, u1 = divmod(j + 1, 8)
            scale = column[g1][u1 : u1 + 1, :] * inverse
            for h in range(g1, groups):
                ahead[h] = jnp.broadcast_to(upper[h][:, j + 1 : j + 2], (8, n)) - column[h] * scale
        for h in range(g, groups):
            below = column[h]
            if h == g:
                below = jnp.where(rows > u, below, 0.0)
            upper[h] = upper[h] - below * row
            ops[h] = ops[h] - below * row_ops
        column = ahead
    return jnp.concatenate(upper, 0), jnp.concatenate(ops, 0)


def factor_kernel(corner, lower, inverse, work, copied, sem, *, tiles, per_col, col_count):
    t = corner.shape[-1]
    rows = lax.broadcasted_iota(jnp.int32, (t, t), 0)
    cols = lax.broadcasted_iota(jnp.int32, (t, t), 1)
    copies = []
    for p in range(tiles):
        for j in range(p + 1):
            copies.append(
                pltpu.make_async_copy(
                    corner.at[p * col_count + j % col_count, j // col_count], copied.at[p, j], sem
                )
            )
    for copy in copies:
        copy.start()
    lower[...] = jnp.zeros_like(lower)
    for copy in copies:
        copy.wait()

    for p in range(tiles):
        for j in range(p + 1):
            block = copied[p, j]
            if p == j:
                block = jnp.where(rows >= cols, block, block.T)
                work[p, :, p * t : (p + 1) * t] = block
            else:
                work[p, :, j * t : (j + 1) * t] = block
                work[j, :, p * t : (p + 1) * t] = block.T

    def step(j, _):
        here = pl.ds(pl.multiple_of(j * t, t), t)
        upper, ops = eliminate(work[j, :, here])
        pivots = jnp.sum(jnp.where(rows == cols, upper, 0.0), 1, keepdims=True)
        scale = lax.rsqrt(pivots)
        upper = jnp.where(rows <= cols, upper * scale, 0.0)
        ops = jnp.where(rows >= cols, ops * scale, 0.0)
        lower[pl.ds(pl.multiple_of(j * t, t), t), here] = upper.T.astype(lower.dtype)
        work[j, :, here] = jnp.where(rows == cols, 1.0, 0.0)
        work[j] = contract(ops, work[j], 1, 0)

        def below(i, _):
            block = contract(work[i, :, here], ops, 1, 1)
            lower[pl.ds(pl.multiple_of(i * t, t), t), here] = block.astype(lower.dtype)
            work[i, :, here] = jnp.zeros((t, t), jnp.float32)
            work[i] = work[i] - contract(block, work[j], 1, 0)
            return 0

        lax.fori_loop(j + 1, tiles, below, 0)
        return 0

    lax.fori_loop(0, tiles, step, 0)
    wide_rows = lax.broadcasted_iota(jnp.int32, (t, tiles * t), 1)
    for p in range(tiles):
        inverse[p * t : (p + 1) * t, :] = jnp.where(wide_rows < (p + 1) * t, work[p], 0.0)


def factor(corner, tiles, per_col, col_count):
    t = corner.shape[-1]
    n = tiles * t
    vmem = pl.BlockSpec(memory_space=pltpu.VMEM)
    return pl.pallas_call(
        functools.partial(factor_kernel, tiles=tiles, per_col=per_col, col_count=col_count),
        in_specs=[pl.BlockSpec(memory_space=ANY)],
        out_specs=[vmem, vmem],
        out_shape=[jax.ShapeDtypeStruct((n, n), jnp.bfloat16), jax.ShapeDtypeStruct((n, n), jnp.float32)],
        scratch_shapes=[
            pltpu.VMEM((tiles, t, n), jnp.float32),
            pltpu.VMEM((tiles, tiles, t, t), jnp.float32),
            pltpu.SemaphoreType.DMA,
        ],
        compiler_params=params(),
        cost_estimate=pl.CostEstimate(flops=100_000_000_000, bytes_accessed=200_000_000, transcendentals=0),
        name="factor_corner",
    )(corner)


def panel_kernel(landing, front, arrived, out, buf, tiles, picked, in_sem, tile_sem, out_sem, *, per_col, col_tiles):
    slots = landing.shape[0]

    def front_copy(s):
        return pltpu.make_async_copy(front.at[:, :, s, :], buf.at[:, s], in_sem)

    for s in range(per_col):
        front_copy(s).start()

    def find(k, n):
        slot = landing[k]
        hit = jnp.logical_and(slot >= 0, lax.rem(slot, col_tiles) < per_col)

        @pl.when(hit)
        def _():
            picked[n] = slot
            pltpu.make_async_copy(arrived.at[k], tiles.at[n], tile_sem).start()

        return n + hit.astype(jnp.int32)

    found = lax.fori_loop(0, slots, find, 0)
    for s in range(per_col):
        front_copy(s).wait()

    def wait(n, _):
        pltpu.make_async_copy(arrived.at[0], tiles.at[0], tile_sem).wait()
        return 0

    lax.fori_loop(0, found, wait, 0)

    def add(n, _):
        q = picked[n] // col_tiles
        s = lax.rem(picked[n], col_tiles)
        buf[q, s] = buf[q, s] + tiles[n].astype(jnp.float32)
        return 0

    lax.fori_loop(0, found, add, 0)
    copy = pltpu.make_async_copy(buf, out, out_sem)
    copy.start()
    copy.wait()


def assemble_panel(landing, front, arrived, per_col):
    row_tiles, t, col_tiles, _ = front.shape
    any_spec = pl.BlockSpec(memory_space=ANY)
    return pl.pallas_call(
        functools.partial(panel_kernel, per_col=per_col, col_tiles=col_tiles),
        in_specs=[pl.BlockSpec(memory_space=pltpu.SMEM), any_spec, any_spec],
        out_specs=any_spec,
        out_shape=jax.ShapeDtypeStruct((row_tiles, per_col, t, t), jnp.float32),
        scratch_shapes=[
            pltpu.VMEM((row_tiles, per_col, t, t), jnp.float32),
            pltpu.VMEM(arrived.shape, arrived.dtype),
            pltpu.SMEM(landing.shape, jnp.int32),
            pltpu.SemaphoreType.DMA,
            pltpu.SemaphoreType.DMA,
            pltpu.SemaphoreType.DMA,
        ],
        compiler_params=params(),
        cost_estimate=pl.CostEstimate(flops=0, bytes_accessed=20_000_000, transcendentals=0),
        name="assemble_panel",
    )(landing, front, arrived)


def update_kernel(
    landing, front, panel, left, right, arrived, out,
    buf, left_v, right_v, tiles, head, following,
    in_sem, out_sem, left_sem, right_sem, tile_sem, panel_sem,
    *, per_col, sub_count, span, depth, together,
):
    row_tiles, t, col_tiles, _ = front.shape
    slots = landing.shape[0]
    steps = row_tiles // span
    wide = col_tiles - per_col

    def read(i, slot, s):
        return pltpu.make_async_copy(
            front.at[pl.ds(i * span, span), :, per_col + s, :], buf.at[slot, s], in_sem.at[slot]
        )

    def write(i, slot, s):
        return pltpu.make_async_copy(
            buf.at[slot, s], out.at[pl.ds(i * span, span), :, per_col + s, :], out_sem.at[slot]
        )

    def read_all(i, slot):
        for s in range(wide):
            read(i, slot, s).start()

    def right_copy(s):
        c = per_col + s
        return pltpu.make_async_copy(
            right.at[c % sub_count, c // sub_count], right_v.at[s], right_sem.at[s // together]
        )

    left_copy = pltpu.make_async_copy(left, left_v, left_sem)
    left_copy.start()
    for s in range(wide):
        right_copy(s).start()
    read_all(0, 0)
    tile_copy = pltpu.make_async_copy(arrived, tiles, tile_sem)
    tile_copy.start()
    panel_copies = [
        pltpu.make_async_copy(panel.at[:, s], out.at[:, :, s, :], panel_sem.at[s]) for s in range(per_col)
    ]

    def clear(q, _):
        head[q] = -1
        return 0

    lax.fori_loop(0, row_tiles, clear, 0)

    def link(k, _):
        slot = landing[k]

        @pl.when(jnp.logical_and(slot >= 0, lax.rem(slot, col_tiles) >= per_col))
        def _():
            q = slot // col_tiles
            following[k] = head[q]
            head[q] = k

        return 0

    lax.fori_loop(0, slots, link, 0)
    left_copy.wait()

    def step(i, _):
        slot = lax.rem(i, depth)

        @pl.when(i + 1 < steps)
        def _():
            later = lax.rem(i + 1, depth)

            @pl.when(i + 1 >= depth)
            def _():
                for s in range(wide):
                    write(0, later, s).wait()

            read_all(i + 1, later)

        rows = left_v[pl.ds(i * span, span)].reshape(span * t, left_v.shape[-1])
        for s in range(wide):
            read(0, slot, s).wait()
        for s in range(0, wide, together):
            @pl.when(i == 0)
            def _():
                for o in range(together):
                    right_copy(s + o).wait()

            cols = right_v[s : s + together].reshape(together * t, right_v.shape[-1])
            product = lax.dot_general(
                rows, cols, (((1,), (1,)), ((), ())), preferred_element_type=jnp.float32
            )
            for o in range(together):
                piece = product[:, o * t : (o + 1) * t].reshape(span, t, t)
                buf[slot, s + o] = buf[slot, s + o] - piece

        @pl.when(i == 0)
        def _():
            tile_copy.wait()
            for copy in panel_copies:
                copy.start()

        for d in range(span):

            def add(k):
                s = lax.rem(landing[k], col_tiles) - per_col
                buf[slot, s, d] = buf[slot, s, d] + tiles[k].astype(jnp.float32)
                return following[k]

            lax.while_loop(lambda k: k >= 0, add, head[i * span + d])

        for s in range(wide):
            write(i, slot, s).start()
        return 0

    lax.fori_loop(0, steps, step, 0)
    for i in range(max(0, steps - depth), steps):
        for s in range(wide):
            write(0, i % depth, s).wait()
    for copy in panel_copies:
        copy.wait()


def update(landing, front, panel, left, right, arrived, per_col):
    row_tiles, t, col_tiles, _ = front.shape
    sub_count = right.shape[0]
    span = 2 if row_tiles % 2 == 0 else 1
    depth = 3
    wide = col_tiles - per_col
    together = 2 if wide % 2 == 0 else 1
    any_spec = pl.BlockSpec(memory_space=ANY)
    return pl.pallas_call(
        functools.partial(
            update_kernel, per_col=per_col, sub_count=sub_count, span=span, depth=depth, together=together
        ),
        in_specs=[pl.BlockSpec(memory_space=pltpu.SMEM)] + [any_spec] * 5,
        out_specs=any_spec,
        out_shape=jax.ShapeDtypeStruct(front.shape, jnp.float32),
        scratch_shapes=[
            pltpu.VMEM((depth, wide, span, t, t), jnp.float32),
            pltpu.VMEM(left.shape, left.dtype),
            pltpu.VMEM((wide, t, left.shape[-1]), right.dtype),
            pltpu.VMEM(arrived.shape, arrived.dtype),
            pltpu.SMEM((row_tiles,), jnp.int32),
            pltpu.SMEM(landing.shape, jnp.int32),
            pltpu.SemaphoreType.DMA((depth,)),
            pltpu.SemaphoreType.DMA((depth,)),
            pltpu.SemaphoreType.DMA,
            pltpu.SemaphoreType.DMA((wide // together,)),
            pltpu.SemaphoreType.DMA,
            pltpu.SemaphoreType.DMA((per_col,)),
        ],
        compiler_params=params(),
        cost_estimate=pl.CostEstimate(
            flops=2 * row_tiles * t * wide * t * left.shape[-1],
            bytes_accessed=2 * front.size * 4,
            transcendentals=0,
        ),
        name="trailing_update",
    )(landing, front, panel, left, right, arrived)


def across_rows(mine, row_index, col_index, row_count, col_count):
    if row_count != 4 or col_count != 4:
        return lax.psum(jnp.where(row_index == col_index, mine, jnp.zeros_like(mine)), "row")
    role = row_index ^ col_index
    half = mine.shape[0] // 2
    first, second = mine[:half], mine[half:]

    def hop(value, moves):
        pairs = []
        for c in range(col_count):
            for a, b in moves:
                pairs.append(((c ^ a) * col_count + c, (c ^ b) * col_count + c))
        return lax.ppermute(value, ("row", "col"), pairs)

    first_1 = hop(first, [(0, 1)])
    second_1 = hop(second, [(0, 2)])
    first_2 = hop(jnp.where(role == 0, first, first_1), [(0, 2), (1, 3)])
    second_2 = hop(jnp.where(role == 0, second, second_1), [(0, 1), (2, 3)])
    first = jnp.where(role == 0, first, jnp.where(role == 1, first_1, first_2))
    second = jnp.where(role == 0, second, jnp.where(role == 2, second_1, second_2))
    return jnp.concatenate([first, second], 0)


def local(front, child_tiles, tile_owner, tile_slot):
    row_tiles, _, t, col_tiles, _, _ = front.shape
    sub_count = lax.axis_size("sub")
    row_count = lax.axis_size("row")
    col_count = lax.axis_size("col")
    dev_count = sub_count * row_count * col_count
    tile_count = child_tiles.shape[0]
    capacity = max(2, 2 * tile_count // dev_count)
    panel_tiles = NB // t
    per_col = panel_tiles // col_count
    part = row_tiles // col_count
    local_front = front.reshape(row_tiles, t, col_tiles, t)
    sub_index = lax.axis_index("sub")
    row_index = lax.axis_index("row")
    col_index = lax.axis_index("col")
    group_id = sub_index * row_count + row_index

    corner = local_front[0, :, :per_col, :].transpose(1, 0, 2)
    corner = lax.all_gather(corner, ("sub", "row", "col"), axis=0)

    outgoing, targets = pack(tile_owner[:, 0], tile_slot, child_tiles, dev_count, capacity)
    landing = lax.all_to_all(
        targets.reshape(dev_count, capacity), ("sub", "row", "col"), split_axis=0, concat_axis=0, tiled=True
    ).reshape(dev_count * capacity)
    arrived = lax.all_to_all(
        outgoing.reshape(dev_count, capacity, t, t), ("sub", "row", "col"), split_axis=0, concat_axis=0, tiled=True
    ).reshape(dev_count * capacity, t, t)
    lower, inverse = factor(corner, panel_tiles, per_col, col_count)

    panel = assemble_panel(landing, local_front, arrived, per_col)
    shared = lax.all_to_all(
        panel.reshape(col_count, part, per_col, t, t), "col", split_axis=0, concat_axis=0, tiled=True
    )
    shared = shared.transpose(1, 3, 2, 0, 4).reshape(part * t, NB)
    solved = contract(shared, inverse, 1, 1).astype(jnp.bfloat16).reshape(part, t, NB)
    leading = lax.dynamic_slice_in_dim(lower, jnp.minimum(group_id, panel_tiles - 1) * t, t, 0)
    is_leading = group_id < panel_tiles
    upper = jnp.where(jnp.logical_and(is_leading, col_index == 0), leading, solved[0])
    solved = jnp.concatenate([upper[None], solved[1:]], 0)
    rows = lax.all_gather(solved, "col", axis=0, tiled=True)
    panel_out = lax.dynamic_index_in_dim(
        rows.reshape(row_tiles, t, per_col, col_count, t), col_index, 3, keepdims=True
    ).reshape(row_tiles, 1, t, per_col, 1, t)
    across = across_rows(rows, row_index, col_index, row_count, col_count)
    right = lax.all_gather(across, "sub", axis=0)
    left = jnp.concatenate([jnp.where(is_leading, jnp.zeros_like(rows[:1]), rows[:1]), rows[1:]], 0)
    result = update(landing, local_front, panel, left, right, arrived, per_col)
    return (result.reshape(front.shape), panel_out)


def solution(mesh):
    return jax.shard_map(
        local,
        mesh=mesh,
        in_specs=(
            P(None, ("sub", "row"), None, None, "col", None),
            P(("sub", "row", "col"), None, None),
            P(("sub", "row", "col"), None),
            P(("sub", "row", "col")),
        ),
        out_specs=(
            P(None, ("sub", "row"), None, None, "col", None),
            P(None, ("sub", "row"), None, None, "col", None),
        ),
        check_vma=False,
    )
```

```python
import functools

import jax
import jax.numpy as jnp
from jax import lax
from jax.experimental import pallas as pl
from jax.experimental.pallas import tpu as pltpu
from jax.sharding import PartitionSpec as P

NB = 1024
ANY = pl.ANY
EXACT = lax.Precision.HIGHEST
VMEM_LIMIT = 56 * 1024 * 1024


def params():
    return pltpu.CompilerParams(vmem_limit_bytes=VMEM_LIMIT)


def contract(a, b, dim_a, dim_b):
    return lax.dot_general(
        a, b, (((dim_a,), (dim_b,)), ((), ())), precision=EXACT, preferred_element_type=jnp.float32
    )


def pack_kernel(owner, slot, tiles, outgoing, targets, counts, held, in_sem, sem, *, capacity):
    tile_count = tiles.shape[0]
    dev_count = counts.shape[0]
    load = pltpu.make_async_copy(tiles, held, in_sem)
    load.start()

    def clear(d, _):
        counts[d] = 0
        for r in range(capacity):
            targets[d * capacity + r] = -1
        return 0

    lax.fori_loop(0, dev_count, clear, 0)
    load.wait()

    def send(k, _):
        d = owner[k]
        place = d * capacity + counts[d]
        counts[d] = counts[d] + 1
        targets[place] = slot[k]
        pltpu.make_async_copy(held.at[k], outgoing.at[place], sem).start()
        return 0

    lax.fori_loop(0, tile_count, send, 0)
    pltpu.make_async_copy(held, outgoing.at[pl.ds(0, tile_count)], sem).wait()


def pack(owner, slot, tiles, dev_count, capacity):
    smem = pl.BlockSpec(memory_space=pltpu.SMEM)
    return pl.pallas_call(
        functools.partial(pack_kernel, capacity=capacity),
        in_specs=[smem, smem, pl.BlockSpec(memory_space=ANY)],
        out_specs=[pl.BlockSpec(memory_space=ANY), smem],
        out_shape=[
            jax.ShapeDtypeStruct((dev_count * capacity,) + tiles.shape[1:], tiles.dtype),
            jax.ShapeDtypeStruct((dev_count * capacity,), jnp.int32),
        ],
        scratch_shapes=[
            pltpu.SMEM((dev_count,), jnp.int32),
            pltpu.VMEM(tiles.shape, tiles.dtype),
            pltpu.SemaphoreType.DMA,
            pltpu.SemaphoreType.DMA,
        ],
        compiler_params=params(),
        cost_estimate=pl.CostEstimate(flops=0, bytes_accessed=2 * tiles.size * 2, transcendentals=0),
        name="pack_children",
    )(owner, slot, tiles)


def eliminate(tile):
    n = tile.shape[0]
    groups = n // 8
    rows = lax.broadcasted_iota(jnp.int32, (8, n), 0)
    lanes = lax.broadcasted_iota(jnp.int32, (8, n), 1)
    upper = [tile[8 * h : 8 * h + 8, :] for h in range(groups)]
    ops = [jnp.where(lanes == rows + 8 * h, 1.0, 0.0).astype(jnp.float32) for h in range(groups)]
    column = [jnp.broadcast_to(upper[h][:, 0:1], (8, n)) for h in range(groups)]
    for j in range(n):
        g, u = divmod(j, 8)
        inverse = 1.0 / column[g][u : u + 1, :]
        row = upper[g][u : u + 1, :] * inverse
        row_ops = ops[g][u : u + 1, :] * inverse
        ahead = [None] * groups
        if j + 1 < n:
            g1, u1 = divmod(j + 1, 8)
            scale = column[g1][u1 : u1 + 1, :] * inverse
            for h in range(g1, groups):
                ahead[h] = jnp.broadcast_to(upper[h][:, j + 1 : j + 2], (8, n)) - column[h] * scale
        for h in range(g, groups):
            below = column[h]
            if h == g:
                below = jnp.where(rows > u, below, 0.0)
            upper[h] = upper[h] - below * row
            ops[h] = ops[h] - below * row_ops
        column = ahead
    return jnp.concatenate(upper, 0), jnp.concatenate(ops, 0)


def factor_kernel(corner, lower, inverse, work, copied, sem, *, tiles, per_col, col_count):
    t = corner.shape[-1]
    rows = lax.broadcasted_iota(jnp.int32, (t, t), 0)
    cols = lax.broadcasted_iota(jnp.int32, (t, t), 1)
    copies = []
    for p in range(tiles):
        for j in range(p + 1):
            copies.append(
                pltpu.make_async_copy(
                    corner.at[p * col_count + j % col_count, j // col_count], copied.at[p, j], sem
                )
            )
    for copy in copies:
        copy.start()
    lower[...] = jnp.zeros_like(lower)
    for copy in copies:
        copy.wait()

    for p in range(tiles):
        for j in range(p + 1):
            block = copied[p, j]
            if p == j:
                block = jnp.where(rows >= cols, block, block.T)
                work[p, :, p * t : (p + 1) * t] = block
            else:
                work[p, :, j * t : (j + 1) * t] = block
                work[j, :, p * t : (p + 1) * t] = block.T

    def step(j, _):
        here = pl.ds(pl.multiple_of(j * t, t), t)
        upper, ops = eliminate(work[j, :, here])
        pivots = jnp.sum(jnp.where(rows == cols, upper, 0.0), 1, keepdims=True)
        scale = lax.rsqrt(pivots)
        upper = jnp.where(rows <= cols, upper * scale, 0.0)
        ops = jnp.where(rows >= cols, ops * scale, 0.0)
        lower[pl.ds(pl.multiple_of(j * t, t), t), here] = upper.T.astype(lower.dtype)
        work[j, :, here] = jnp.where(rows == cols, 1.0, 0.0)
        work[j] = contract(ops, work[j], 1, 0)

        def below(i, _):
            block = contract(work[i, :, here], ops, 1, 1)
            lower[pl.ds(pl.multiple_of(i * t, t), t), here] = block.astype(lower.dtype)
            work[i, :, here] = jnp.zeros((t, t), jnp.float32)
            work[i] = work[i] - contract(block, work[j], 1, 0)
            return 0

        lax.fori_loop(j + 1, tiles, below, 0)
        return 0

    lax.fori_loop(0, tiles, step, 0)
    wide_rows = lax.broadcasted_iota(jnp.int32, (t, tiles * t), 1)
    for p in range(tiles):
        inverse[p * t : (p + 1) * t, :] = jnp.where(wide_rows < (p + 1) * t, work[p], 0.0)


def factor(corner, tiles, per_col, col_count):
    t = corner.shape[-1]
    n = tiles * t
    vmem = pl.BlockSpec(memory_space=pltpu.VMEM)
    return pl.pallas_call(
        functools.partial(factor_kernel, tiles=tiles, per_col=per_col, col_count=col_count),
        in_specs=[pl.BlockSpec(memory_space=ANY)],
        out_specs=[vmem, vmem],
        out_shape=[jax.ShapeDtypeStruct((n, n), jnp.bfloat16), jax.ShapeDtypeStruct((n, n), jnp.float32)],
        scratch_shapes=[
            pltpu.VMEM((tiles, t, n), jnp.float32),
            pltpu.VMEM((tiles, tiles, t, t), jnp.float32),
            pltpu.SemaphoreType.DMA,
        ],
        compiler_params=params(),
        cost_estimate=pl.CostEstimate(flops=100_000_000_000, bytes_accessed=200_000_000, transcendentals=0),
        name="factor_corner",
    )(corner)


def panel_kernel(landing, front, arrived, out, buf, tiles, picked, in_sem, tile_sem, out_sem, *, per_col, col_tiles):
    slots = landing.shape[0]

    def front_copy(s):
        return pltpu.make_async_copy(front.at[:, :, s, :], buf.at[:, s], in_sem)

    for s in range(per_col):
        front_copy(s).start()

    def find(k, n):
        slot = landing[k]
        hit = jnp.logical_and(slot >= 0, lax.rem(slot, col_tiles) < per_col)

        @pl.when(hit)
        def _():
            picked[n] = slot
            pltpu.make_async_copy(arrived.at[k], tiles.at[n], tile_sem).start()

        return n + hit.astype(jnp.int32)

    found = lax.fori_loop(0, slots, find, 0)
    for s in range(per_col):
        front_copy(s).wait()

    def wait(n, _):
        pltpu.make_async_copy(arrived.at[0], tiles.at[0], tile_sem).wait()
        return 0

    lax.fori_loop(0, found, wait, 0)

    def add(n, _):
        q = picked[n] // col_tiles
        s = lax.rem(picked[n], col_tiles)
        buf[q, s] = buf[q, s] + tiles[n].astype(jnp.float32)
        return 0

    lax.fori_loop(0, found, add, 0)
    copy = pltpu.make_async_copy(buf, out, out_sem)
    copy.start()
    copy.wait()


def assemble_panel(landing, front, arrived, per_col):
    row_tiles, t, col_tiles, _ = front.shape
    any_spec = pl.BlockSpec(memory_space=ANY)
    return pl.pallas_call(
        functools.partial(panel_kernel, per_col=per_col, col_tiles=col_tiles),
        in_specs=[pl.BlockSpec(memory_space=pltpu.SMEM), any_spec, any_spec],
        out_specs=any_spec,
        out_shape=jax.ShapeDtypeStruct((row_tiles, per_col, t, t), jnp.float32),
        scratch_shapes=[
            pltpu.VMEM((row_tiles, per_col, t, t), jnp.float32),
            pltpu.VMEM(arrived.shape, arrived.dtype),
            pltpu.SMEM(landing.shape, jnp.int32),
            pltpu.SemaphoreType.DMA,
            pltpu.SemaphoreType.DMA,
            pltpu.SemaphoreType.DMA,
        ],
        compiler_params=params(),
        cost_estimate=pl.CostEstimate(flops=0, bytes_accessed=20_000_000, transcendentals=0),
        name="assemble_panel",
    )(landing, front, arrived)


def update_kernel(
    landing, place, front, panel, arrived, *rest,
    per_col, sub_count, span, depth, together, lines, rounds,
):
    left, rest = rest[:lines], rest[lines:]
    right, rest = rest[:rounds * sub_count], rest[rounds * sub_count :]
    out, buf, left_v, right_v, tiles, head, following = rest[:7]
    in_sem, out_sem, left_sem, right_sem, tile_sem = rest[7:]
    row_tiles, t, col_tiles, _ = front.shape
    slots = landing.shape[0]
    steps = row_tiles // span
    wide = col_tiles - per_col

    def read(i, slot, s):
        here = pl.ds(i * span, span)
        source = panel.at[here, s] if s < per_col else front.at[here, :, s, :]
        return pltpu.make_async_copy(source, buf.at[slot, s], in_sem.at[slot])

    def write(i, slot, s):
        return pltpu.make_async_copy(
            buf.at[slot, s], out.at[pl.ds(i * span, span), :, s, :], out_sem.at[slot]
        )

    def read_all(i, slot):
        for s in range(col_tiles):
            read(i, slot, s).start()

    part = left[0].shape[0]
    count = row_tiles // part
    for k in range(count):
        for c in range(count):

            @pl.when(place[0] == c)
            def _(k=k, c=c):
                piece = left[c - k] if k <= c else left[count - 1 + k - c]
                pltpu.make_async_copy(piece, left_v.at[pl.ds(k * part, part)], left_sem).start()

    for n in range(rounds):
        for i in range(sub_count):
            origin = lax.rem(place[1] + sub_count - i, sub_count)
            for r in range(part):
                column = (place[3 + n] * part + r) * sub_count + origin

                @pl.when(column >= per_col)
                def _(n=n, i=i, r=r, column=column):
                    pltpu.make_async_copy(
                        right[n * sub_count + i].at[r], right_v.at[column - per_col], right_sem
                    ).start()

    read_all(0, 0)
    tile_copy = pltpu.make_async_copy(arrived, tiles, tile_sem)

    def clear(q, _):
        head[q] = -1
        return 0

    lax.fori_loop(0, row_tiles, clear, 0)

    def link(k, _):
        slot = landing[k]

        @pl.when(jnp.logical_and(slot >= 0, lax.rem(slot, col_tiles) >= per_col))
        def _():
            q = slot // col_tiles
            following[k] = head[q]
            head[q] = k

        return 0

    lax.fori_loop(0, slots, link, 0)
    pltpu.make_async_copy(left_v, left_v, left_sem).wait()

    @pl.when(place[2] == 1)
    def _():
        left_v[0] = jnp.zeros_like(left_v[0])

    pltpu.make_async_copy(right_v, right_v, right_sem).wait()

    def step(i, _):
        slot = lax.rem(i, depth)

        @pl.when(i + 1 < steps)
        def _():
            later = lax.rem(i + 1, depth)

            @pl.when(i + 1 >= depth)
            def _():
                for s in range(col_tiles):
                    write(0, later, s).wait()

            read_all(i + 1, later)

        @pl.when(i == 0)
        def _():
            tile_copy.start()

        rows = left_v[pl.ds(i * span, span)].reshape(span * t, left_v.shape[-1])
        for s in range(col_tiles):
            read(0, slot, s).wait()
        for s in range(0, wide, together):
            cols = right_v[s : s + together].reshape(together * t, right_v.shape[-1])
            product = lax.dot_general(
                rows, cols, (((1,), (1,)), ((), ())), preferred_element_type=jnp.float32
            )
            for o in range(together):
                piece = product[:, o * t : (o + 1) * t].reshape(span, t, t)
                buf[slot, per_col + s + o] = buf[slot, per_col + s + o] - piece

        @pl.when(i == 0)
        def _():
            tile_copy.wait()

        for d in range(span):

            def add(k):
                s = lax.rem(landing[k], col_tiles)
                buf[slot, s, d] = buf[slot, s, d] + tiles[k].astype(jnp.float32)
                return following[k]

            lax.while_loop(lambda k: k >= 0, add, head[i * span + d])

        for s in range(col_tiles):
            write(i, slot, s).start()
        return 0

    lax.fori_loop(0, steps, step, 0)
    for i in range(max(0, steps - depth), steps):
        for s in range(col_tiles):
            write(0, i % depth, s).wait()


def update(landing, place, front, panel, arrived, left, right, sub_count, per_col):
    row_tiles, t, col_tiles, _ = front.shape
    span = 2 if row_tiles % 2 == 0 else 1
    depth = 3
    wide = col_tiles - per_col
    together = max(d for d in range(1, 11) if wide % d == 0)
    width = left[0].shape[-1]
    any_spec = pl.BlockSpec(memory_space=ANY)
    smem = pl.BlockSpec(memory_space=pltpu.SMEM)
    return pl.pallas_call(
        functools.partial(
            update_kernel,
            per_col=per_col,
            sub_count=sub_count,
            span=span,
            depth=depth,
            together=together,
            lines=len(left),
            rounds=len(right) // sub_count,
        ),
        in_specs=[smem, smem] + [any_spec] * (3 + len(left) + len(right)),
        out_specs=any_spec,
        out_shape=jax.ShapeDtypeStruct(front.shape, jnp.float32),
        scratch_shapes=[
            pltpu.VMEM((depth, col_tiles, span, t, t), jnp.float32),
            pltpu.VMEM((row_tiles, t, width), jnp.bfloat16),
            pltpu.VMEM((wide, t, width), jnp.bfloat16),
            pltpu.VMEM(arrived.shape, arrived.dtype),
            pltpu.SMEM((row_tiles,), jnp.int32),
            pltpu.SMEM(landing.shape, jnp.int32),
            pltpu.SemaphoreType.DMA((depth,)),
            pltpu.SemaphoreType.DMA((depth,)),
            pltpu.SemaphoreType.DMA,
            pltpu.SemaphoreType.DMA,
            pltpu.SemaphoreType.DMA,
        ],
        compiler_params=params(),
        cost_estimate=pl.CostEstimate(
            flops=2 * row_tiles * t * wide * t * width, bytes_accessed=2 * front.size * 4, transcendentals=0
        ),
        name="trailing_update",
    )(landing, place, front, panel, arrived, *left, *right)


def tie(*values):
    return lax.optimization_barrier(values)


def nearest_first(c, count):
    return sorted(range(count), key=lambda k: (abs(k - c), k))


def exchange(own, row_index, col_index, row_count, col_count, sub_count):
    half = own.shape[0] // 2
    spread = row_count == 4 and col_count == 4 and half > 0
    role = row_index ^ col_index
    orders = [nearest_first(c, col_count) for c in range(col_count)]
    up, down, right = [own], [own], []

    def along(value, step, first, last):
        pairs = [(c, c + step) for c in range(first, last) if 0 <= c + step < col_count]
        return lax.ppermute(value, "col", pairs)

    def hop(value, moves):
        pairs = []
        for c in range(col_count):
            for a, b in moves:
                pairs.append(((c ^ a) * col_count + c, (c ^ b) * col_count + c))
        return lax.ppermute(value, ("row", "col"), pairs)

    for n in range(col_count):
        source = own
        if n > 0:
            for c in range(col_count):
                k = orders[c][n]
                piece = up[c - k] if k < c else down[k - c]
                source = piece if c == 0 else jnp.where(col_index == c, piece, source)
        lines = []
        if n + 1 < col_count:
            lines = [along(up[n], 1, n, col_count), along(down[n], -1, 0, col_count - n)]
        if spread:
            first, second = source[:half], source[half:]
            first_1, second_1 = tie(hop(first, [(0, 1)]), hop(second, [(0, 2)]))
            first_2 = hop(jnp.where(role == 0, first, first_1), [(0, 2), (1, 3)])
            second_2 = hop(jnp.where(role == 0, second, second_1), [(0, 1), (2, 3)])
            first_2, second_2, *lines = tie(first_2, second_2, *lines)
            whole = jnp.concatenate(
                [
                    jnp.where(role == 0, first, jnp.where(role == 1, first_1, first_2)),
                    jnp.where(role == 0, second, jnp.where(role == 2, second_1, second_2)),
                ],
                0,
            )
        else:
            whole = lax.psum(jnp.where(row_index == col_index, source, jnp.zeros_like(source)), "row")
        if lines:
            up.append(lines[0])
            down.append(lines[1])
        right.append(whole)
        for i in range(1, sub_count):
            right.append(lax.ppermute(whole, "sub", [(s, (s + i) % sub_count) for s in range(sub_count)]))
    return up, down[1:], right


def local(front, child_tiles, tile_owner, tile_slot):
    row_tiles, _, t, col_tiles, _, _ = front.shape
    sub_count = lax.axis_size("sub")
    row_count = lax.axis_size("row")
    col_count = lax.axis_size("col")
    dev_count = sub_count * row_count * col_count
    tile_count = child_tiles.shape[0]
    capacity = max(2, 2 * tile_count // dev_count)
    panel_tiles = NB // t
    per_col = panel_tiles // col_count
    part = row_tiles // col_count
    local_front = front.reshape(row_tiles, t, col_tiles, t)
    sub_index = lax.axis_index("sub")
    row_index = lax.axis_index("row")
    col_index = lax.axis_index("col")
    group_id = sub_index * row_count + row_index

    corner = local_front[0, :, :per_col, :].transpose(1, 0, 2)
    corner, child_tiles = tie(corner, child_tiles)
    corner = lax.all_gather(corner, ("sub", "row", "col"), axis=0)

    outgoing, targets = pack(tile_owner[:, 0], tile_slot, child_tiles, dev_count, capacity)
    landing = lax.all_to_all(
        targets.reshape(dev_count, capacity), ("sub", "row", "col"), split_axis=0, concat_axis=0, tiled=True
    ).reshape(dev_count * capacity)
    arrived = lax.all_to_all(
        outgoing.reshape(dev_count, capacity, t, t), ("sub", "row", "col"), split_axis=0, concat_axis=0, tiled=True
    ).reshape(dev_count * capacity, t, t)
    lower, inverse = factor(corner, panel_tiles, per_col, col_count)
    arrived, landing, lower, inverse = tie(arrived, landing, lower, inverse)

    panel = assemble_panel(landing, local_front, arrived, per_col)
    shared = lax.all_to_all(
        panel.reshape(col_count, part, per_col, t, t), "col", split_axis=0, concat_axis=0, tiled=True
    )
    shared = shared.transpose(1, 3, 2, 0, 4).reshape(part * t, NB)
    solved = contract(shared, inverse, 1, 1).astype(jnp.bfloat16).reshape(part, t, NB)
    leading = lax.dynamic_slice_in_dim(lower, jnp.minimum(group_id, panel_tiles - 1) * t, t, 0)
    is_leading = group_id < panel_tiles
    upper = jnp.where(jnp.logical_and(is_leading, col_index == 0), leading, solved[0])
    solved = jnp.concatenate([upper[None], solved[1:]], 0)
    up, down, right = exchange(solved, row_index, col_index, row_count, col_count, sub_count)

    mine = []
    for piece in up + down:
        columns = lax.dynamic_index_in_dim(
            piece.reshape(part, t, per_col, col_count, t), col_index, 3, keepdims=False
        )
        mine.append(columns)
    ordered = []
    for k in range(col_count):
        rows = mine[0]
        for c in range(col_count):
            if c != k:
                rows = jnp.where(col_index == c, mine[c - k] if k < c else mine[col_count - 1 + k - c], rows)
        ordered.append(rows)
    panel_out = jnp.concatenate(ordered, 0).reshape(row_tiles, 1, t, per_col, 1, t)

    orders = jnp.array([nearest_first(c, col_count) for c in range(col_count)], jnp.int32)
    place = jnp.concatenate(
        [
            jnp.stack([col_index, sub_index, is_leading.astype(jnp.int32)]).astype(jnp.int32),
            lax.dynamic_index_in_dim(orders, col_index, 0, keepdims=False),
        ]
    )
    result = update(landing, place, local_front, panel, arrived, up + down, right, sub_count, per_col)
    return (result.reshape(front.shape), panel_out)


def solution(mesh):
    return jax.shard_map(
        local,
        mesh=mesh,
        in_specs=(
            P(None, ("sub", "row"), None, None, "col", None),
            P(("sub", "row", "col"), None, None),
            P(("sub", "row", "col"), None),
            P(("sub", "row", "col")),
        ),
        out_specs=(
            P(None, ("sub", "row"), None, None, "col", None),
            P(None, ("sub", "row"), None, None, "col", None),
        ),
        check_vma=False,
    )
```

```python
import functools

import jax
import jax.numpy as jnp
from jax import lax
from jax.experimental import pallas as pl
from jax.experimental.pallas import tpu as pltpu
from jax.sharding import PartitionSpec as P

NB = 1024
ANY = pl.ANY
EXACT = lax.Precision.HIGHEST
VMEM_LIMIT = 56 * 1024 * 1024


def params():
    return pltpu.CompilerParams(vmem_limit_bytes=VMEM_LIMIT)


def contract(a, b, dim_a, dim_b):
    return lax.dot_general(
        a, b, (((dim_a,), (dim_b,)), ((), ())), precision=EXACT, preferred_element_type=jnp.float32
    )


def pack_kernel(owner, slot, tiles, first, second, targets, counts, held, in_sem, sem, *, cut, per_col, col_tiles):
    tile_count = tiles.shape[0]
    dev_count = counts.shape[0]
    late = second.shape[0] // dev_count
    load = pltpu.make_async_copy(tiles, held, in_sem)
    load.start()

    def clear(d, _):
        counts[d] = 0
        for r in range(cut + late):
            targets[d * (cut + late) + r] = -1
        return 0

    lax.fori_loop(0, dev_count, clear, 0)
    load.wait()

    def send(k, lost, panel):
        chosen = lax.rem(slot[k], col_tiles) < per_col
        chosen = chosen if panel else jnp.logical_not(chosen)
        d = owner[k]
        rank = counts[d]

        @pl.when(chosen)
        def _():
            counts[d] = rank + 1
            targets[d * (cut + late) + rank] = slot[k]

            @pl.when(rank < cut)
            def _():
                pltpu.make_async_copy(held.at[k], first.at[d * cut + rank], sem).start()

            @pl.when(rank >= cut)
            def _():
                pltpu.make_async_copy(held.at[k], second.at[d * late + rank - cut], sem).start()

        return lost + jnp.logical_and(chosen, rank >= cut).astype(jnp.int32)

    targets[dev_count * (cut + late)] = lax.fori_loop(0, tile_count, functools.partial(send, panel=True), 0)
    lax.fori_loop(0, tile_count, functools.partial(send, panel=False), 0)
    pltpu.make_async_copy(held, held, sem).wait()


def pack(owner, slot, tiles, dev_count, cut, late, per_col, col_tiles):
    smem = pl.BlockSpec(memory_space=pltpu.SMEM)
    any_spec = pl.BlockSpec(memory_space=ANY)
    return pl.pallas_call(
        functools.partial(pack_kernel, cut=cut, per_col=per_col, col_tiles=col_tiles),
        in_specs=[smem, smem, any_spec],
        out_specs=[any_spec, any_spec, smem],
        out_shape=[
            jax.ShapeDtypeStruct((dev_count * cut,) + tiles.shape[1:], tiles.dtype),
            jax.ShapeDtypeStruct((dev_count * late,) + tiles.shape[1:], tiles.dtype),
            jax.ShapeDtypeStruct((dev_count * (cut + late) + 1,), jnp.int32),
        ],
        scratch_shapes=[
            pltpu.SMEM((dev_count,), jnp.int32),
            pltpu.VMEM(tiles.shape, tiles.dtype),
            pltpu.SemaphoreType.DMA,
            pltpu.SemaphoreType.DMA,
        ],
        compiler_params=params(),
        cost_estimate=pl.CostEstimate(flops=0, bytes_accessed=20_000_000, transcendentals=0),
        name="pack_children",
    )(owner, slot, tiles)


def eliminate(tile):
    n = tile.shape[0]
    groups = n // 8
    rows = lax.broadcasted_iota(jnp.int32, (8, n), 0)
    lanes = lax.broadcasted_iota(jnp.int32, (8, n), 1)
    upper = [tile[8 * h : 8 * h + 8, :] for h in range(groups)]
    ops = [jnp.where(lanes == rows + 8 * h, 1.0, 0.0).astype(jnp.float32) for h in range(groups)]
    column = [jnp.broadcast_to(upper[h][:, 0:1], (8, n)) for h in range(groups)]
    for j in range(n):
        g, u = divmod(j, 8)
        inverse = 1.0 / column[g][u : u + 1, :]
        row = upper[g][u : u + 1, :] * inverse
        row_ops = ops[g][u : u + 1, :] * inverse
        ahead = [None] * groups
        if j + 1 < n:
            g1, u1 = divmod(j + 1, 8)
            scale = column[g1][u1 : u1 + 1, :] * inverse
            for h in range(g1, groups):
                ahead[h] = jnp.broadcast_to(upper[h][:, j + 1 : j + 2], (8, n)) - column[h] * scale
        for h in range(g, groups):
            below = column[h]
            if h == g:
                below = jnp.where(rows > u, below, 0.0)
            upper[h] = upper[h] - below * row
            ops[h] = ops[h] - below * row_ops
        column = ahead
    return jnp.concatenate(upper, 0), jnp.concatenate(ops, 0)


def factor_kernel(corner, lower, inverse, work, copied, sem, *, tiles, per_col, col_count):
    t = corner.shape[-1]
    rows = lax.broadcasted_iota(jnp.int32, (t, t), 0)
    cols = lax.broadcasted_iota(jnp.int32, (t, t), 1)
    copies = []
    for p in range(tiles):
        for j in range(p + 1):
            copies.append(
                pltpu.make_async_copy(
                    corner.at[p * col_count + j % col_count, j // col_count], copied.at[p, j], sem
                )
            )
    for copy in copies:
        copy.start()
    lower[...] = jnp.zeros_like(lower)
    for copy in copies:
        copy.wait()

    for p in range(tiles):
        for j in range(p + 1):
            block = copied[p, j]
            if p == j:
                block = jnp.where(rows >= cols, block, block.T)
                work[p, :, p * t : (p + 1) * t] = block
            else:
                work[p, :, j * t : (j + 1) * t] = block
                work[j, :, p * t : (p + 1) * t] = block.T

    def step(j, _):
        here = pl.ds(pl.multiple_of(j * t, t), t)
        upper, ops = eliminate(work[j, :, here])
        pivots = jnp.sum(jnp.where(rows == cols, upper, 0.0), 1, keepdims=True)
        scale = lax.rsqrt(pivots)
        upper = jnp.where(rows <= cols, upper * scale, 0.0)
        ops = jnp.where(rows >= cols, ops * scale, 0.0)
        lower[pl.ds(pl.multiple_of(j * t, t), t), here] = upper.T.astype(lower.dtype)
        work[j, :, here] = jnp.where(rows == cols, 1.0, 0.0)
        work[j] = contract(ops, work[j], 1, 0)

        def below(i, _):
            block = contract(work[i, :, here], ops, 1, 1)
            lower[pl.ds(pl.multiple_of(i * t, t), t), here] = block.astype(lower.dtype)
            work[i, :, here] = jnp.zeros((t, t), jnp.float32)
            work[i] = work[i] - contract(block, work[j], 1, 0)
            return 0

        lax.fori_loop(j + 1, tiles, below, 0)
        return 0

    lax.fori_loop(0, tiles, step, 0)
    wide_rows = lax.broadcasted_iota(jnp.int32, (t, tiles * t), 1)
    for p in range(tiles):
        inverse[p * t : (p + 1) * t, :] = jnp.where(wide_rows < (p + 1) * t, work[p], 0.0)


def factor(corner, tiles, per_col, col_count):
    t = corner.shape[-1]
    n = tiles * t
    vmem = pl.BlockSpec(memory_space=pltpu.VMEM)
    return pl.pallas_call(
        functools.partial(factor_kernel, tiles=tiles, per_col=per_col, col_count=col_count),
        in_specs=[pl.BlockSpec(memory_space=ANY)],
        out_specs=[vmem, vmem],
        out_shape=[jax.ShapeDtypeStruct((n, n), jnp.bfloat16), jax.ShapeDtypeStruct((n, n), jnp.float32)],
        scratch_shapes=[
            pltpu.VMEM((tiles, t, n), jnp.float32),
            pltpu.VMEM((tiles, tiles, t, t), jnp.float32),
            pltpu.SemaphoreType.DMA,
        ],
        compiler_params=params(),
        cost_estimate=pl.CostEstimate(flops=100_000_000_000, bytes_accessed=200_000_000, transcendentals=0),
        name="factor_corner",
    )(corner)


def corner_kernel(front, out, held, in_sem, out_sem):
    per_col = out.shape[0]
    copies = [pltpu.make_async_copy(front.at[0, :, s, :], held.at[s], in_sem.at[s]) for s in range(per_col)]
    for copy in copies:
        copy.start()
    for copy in copies:
        copy.wait()
    copy = pltpu.make_async_copy(held, out, out_sem)
    copy.start()
    copy.wait()


def take_corner(front, per_col):
    _, t, _, _ = front.shape
    any_spec = pl.BlockSpec(memory_space=ANY)
    return pl.pallas_call(
        corner_kernel,
        in_specs=[any_spec],
        out_specs=any_spec,
        out_shape=jax.ShapeDtypeStruct((per_col, t, t), front.dtype),
        scratch_shapes=[
            pltpu.VMEM((per_col, t, t), front.dtype),
            pltpu.SemaphoreType.DMA((per_col,)),
            pltpu.SemaphoreType.DMA,
        ],
        compiler_params=params(),
        cost_estimate=pl.CostEstimate(flops=0, bytes_accessed=500_000, transcendentals=0),
        name="take_corner",
    )(front)


def panel_kernel(landing, front, arrived, out, buf, tiles, picked, in_sem, tile_sem, out_sem, *, per_col, col_tiles):
    slots = landing.shape[0]

    def front_copy(s):
        return pltpu.make_async_copy(front.at[:, :, s, :], buf.at[:, s], in_sem)

    for s in range(per_col):
        front_copy(s).start()

    def find(k, n):
        slot = landing[k]
        hit = jnp.logical_and(slot >= 0, lax.rem(slot, col_tiles) < per_col)

        @pl.when(hit)
        def _():
            picked[n] = slot
            pltpu.make_async_copy(arrived.at[k], tiles.at[n], tile_sem).start()

        return n + hit.astype(jnp.int32)

    found = lax.fori_loop(0, slots, find, 0)
    for s in range(per_col):
        front_copy(s).wait()

    def wait(n, _):
        pltpu.make_async_copy(arrived.at[0], tiles.at[0], tile_sem).wait()
        return 0

    lax.fori_loop(0, found, wait, 0)

    def add(n, _):
        q = picked[n] // col_tiles
        s = lax.rem(picked[n], col_tiles)
        buf[q, s] = buf[q, s] + tiles[n].astype(jnp.float32)
        return 0

    lax.fori_loop(0, found, add, 0)
    copy = pltpu.make_async_copy(buf, out, out_sem)
    copy.start()
    copy.wait()


def assemble_panel(landing, front, arrived, per_col):
    row_tiles, t, col_tiles, _ = front.shape
    any_spec = pl.BlockSpec(memory_space=ANY)
    return pl.pallas_call(
        functools.partial(panel_kernel, per_col=per_col, col_tiles=col_tiles),
        in_specs=[pl.BlockSpec(memory_space=pltpu.SMEM), any_spec, any_spec],
        out_specs=any_spec,
        out_shape=jax.ShapeDtypeStruct((row_tiles, per_col, t, t), jnp.float32),
        scratch_shapes=[
            pltpu.VMEM((row_tiles, per_col, t, t), jnp.float32),
            pltpu.VMEM(arrived.shape, arrived.dtype),
            pltpu.SMEM(landing.shape, jnp.int32),
            pltpu.SemaphoreType.DMA,
            pltpu.SemaphoreType.DMA,
            pltpu.SemaphoreType.DMA,
        ],
        compiler_params=params(),
        cost_estimate=pl.CostEstimate(flops=0, bytes_accessed=20_000_000, transcendentals=0),
        name="assemble_panel",
    )(landing, front, arrived)


def solve_kernel(where, inverse, lower, *rest, col_count):
    pieces, rest = rest[:col_count], rest[col_count:]
    solved, rows, inverse_v, lead, sem, inv_sem, lead_sem = rest
    part, per_col, t, _ = pieces[0].shape
    for i in range(col_count):
        origin = where[2 + i]
        for q in range(part):
            for s in range(per_col):
                column = pl.multiple_of((s * col_count + origin) * t, t)
                pltpu.make_async_copy(
                    pieces[i].at[q, s], rows.at[pl.ds(q * t, t), pl.ds(column, t)], sem
                ).start()
    inv_copy = pltpu.make_async_copy(inverse, inverse_v, inv_sem)
    inv_copy.start()
    lead_copy = pltpu.make_async_copy(lower.at[pl.ds(where[1] * t, t)], lead, lead_sem)
    lead_copy.start()
    pltpu.make_async_copy(rows, rows, sem).wait()
    inv_copy.wait()
    lead_copy.wait()
    n = inverse.shape[0]
    step = 2 * t if n % (2 * t) == 0 else t
    for b in range(0, n, step):
        product = contract(rows[:, : b + step], inverse_v[b : b + step, : b + step], 1, 1)
        solved[:, b : b + step] = product.astype(solved.dtype)

    @pl.when(where[0] == 1)
    def _():
        solved[:t, :] = lead[...]


def solve(where, pieces, inverse, lower):
    part, _, t, _ = pieces[0].shape
    n = inverse.shape[0]
    any_spec = pl.BlockSpec(memory_space=ANY)
    return pl.pallas_call(
        functools.partial(solve_kernel, col_count=len(pieces)),
        in_specs=[pl.BlockSpec(memory_space=pltpu.SMEM)] + [any_spec] * (2 + len(pieces)),
        out_specs=pl.BlockSpec(memory_space=pltpu.VMEM),
        out_shape=jax.ShapeDtypeStruct((part * t, n), jnp.bfloat16),
        scratch_shapes=[
            pltpu.VMEM((part * t, n), jnp.float32),
            pltpu.VMEM((n, n), jnp.float32),
            pltpu.VMEM((t, n), jnp.bfloat16),
            pltpu.SemaphoreType.DMA,
            pltpu.SemaphoreType.DMA,
            pltpu.SemaphoreType.DMA,
        ],
        compiler_params=params(),
        cost_estimate=pl.CostEstimate(flops=8_000_000_000, bytes_accessed=12_000_000, transcendentals=0),
        name="solve_rows",
    )(where, inverse, lower, *pieces)


def update_kernel(
    area, spot, place, table, front, arrived, arrived_late, *rest,
    blocks, orders, per_col, sub_count, depth, reach, aliased,
):
    row_used = sorted({i for i, _ in blocks})
    col_used = sorted({j for _, j in blocks})
    ups, rest = rest[:reach], rest[reach:]
    downs, rest = rest[:reach], rest[reach:]
    right, rest = rest[: len(col_used) * sub_count], rest[len(col_used) * sub_count :]
    rest = rest[1:] if aliased else rest
    out, token, buf, left_v, right_v, tiles, picked, head, following, lookup = rest[:10]
    in_sem, out_sem, left_sem, right_sem, tile_sem = rest[10:]
    token[...] = jnp.zeros_like(token)
    early = arrived.shape[0]
    t = front.shape[1]
    slots = area.shape[0]
    steps = len(blocks)
    part = ups[0].shape[0]
    count = len(orders)
    width = part * sub_count

    def corner_of(b):
        return place[3 + table[4 * b]], place[3 + table[4 * b + 1]]

    def read(b, slot):
        rows, cols = corner_of(b)
        for j in range(width):
            source = front.at[pl.ds(rows * part, part), :, cols * width + j, :]
            pltpu.make_async_copy(source, buf.at[slot, j], in_sem.at[slot]).start()

    def write(b, slot):
        rows, cols = corner_of(b)
        for j in range(width):
            target = out.at[pl.ds(rows * part, part), :, cols * width + j, :]
            pltpu.make_async_copy(buf.at[slot, j], target, out_sem.at[slot]).start()

    def drain(slot, sem):
        pltpu.make_async_copy(buf.at[slot], buf.at[slot], sem.at[slot]).wait()

    for n, i in enumerate(row_used):
        for c in range(count):
            k = orders[c][i]

            @pl.when(place[0] == c)
            def _(n=n, c=c, k=k):
                piece = ups[c - k] if k <= c else downs[k - c]
                pltpu.make_async_copy(piece, left_v.at[n], left_sem).start()

    for n in range(len(col_used)):
        for i in range(sub_count):
            origin = lax.rem(place[1] + sub_count - i, sub_count)
            for r in range(part):
                pltpu.make_async_copy(
                    right[n * sub_count + i].at[r], right_v.at[n, r * sub_count + origin], right_sem
                ).start()
    for b in range(min(depth - 1, steps)):
        read(b, b)

    for k in range(count * count + 1):
        lookup[k] = -1
    for b in range(steps):
        head[b] = -1
        rows, cols = corner_of(b)
        lookup[rows * count + cols] = b

    def find(k, n):
        b = lookup[area[k]]
        hit = b >= 0

        @pl.when(hit)
        def _():
            picked[n] = spot[k]
            following[n] = head[b]
            head[b] = n

            @pl.when(k < early)
            def _():
                pltpu.make_async_copy(arrived.at[k], tiles.at[n], tile_sem).start()

            @pl.when(k >= early)
            def _():
                pltpu.make_async_copy(arrived_late.at[k - early], tiles.at[n], tile_sem).start()

        return n + hit.astype(jnp.int32)

    found = lax.fori_loop(0, slots, find, 0)
    pltpu.make_async_copy(left_v, left_v, left_sem).wait()
    for n, i in enumerate(row_used):

        @pl.when(jnp.logical_and(place[2] == 1, place[3 + i] == 0))
        def _(n=n):
            left_v[n, 0] = jnp.zeros_like(left_v[n, 0])

    pltpu.make_async_copy(right_v, right_v, right_sem).wait()
    for n, j in enumerate(col_used):

        @pl.when(place[3 + j] == 0)
        def _(n=n):
            right_v[n, :per_col] = jnp.zeros_like(right_v[n, :per_col])

    def wait_tile(n, _):
        pltpu.make_async_copy(arrived.at[0], tiles.at[0], tile_sem).wait()
        return 0

    lax.fori_loop(0, found, wait_tile, 0)

    def step(b, _):
        slot = lax.rem(b, depth)

        @pl.when(b + depth - 1 < steps)
        def _():
            later = lax.rem(b + depth - 1, depth)

            @pl.when(b >= 1)
            def _():
                drain(later, out_sem)

            read(b + depth - 1, later)

        drain(slot, in_sem)
        rows = left_v[table[4 * b + 2]].reshape(part * t, left_v.shape[-1])
        cols = right_v[table[4 * b + 3]].reshape(width * t, right_v.shape[-1])
        product = lax.dot_general(rows, cols, (((1,), (1,)), ((), ())), preferred_element_type=jnp.float32)
        for j in range(width):
            piece = product[:, j * t : (j + 1) * t].reshape(part, t, t)
            buf[slot, j] = buf[slot, j] - piece

        def add(n):
            j, q = lax.rem(picked[n], width), lax.div(picked[n], width)
            buf[slot, j, q] = buf[slot, j, q] + tiles[n].astype(jnp.float32)
            return following[n]

        lax.while_loop(lambda n: n >= 0, add, head[b])
        write(b, slot)
        return 0

    lax.fori_loop(0, steps, step, 0)
    for b in range(max(0, steps - depth), steps):
        drain(b % depth, out_sem)


def update(area, spot, place, front, arrived, arrived_late, up, down, right, so_far, blocks, orders, per_col):
    t = front.shape[1]
    sub_count = len(right[0])
    part, _, inner = up[0].shape
    width = part * sub_count
    count = len(orders)
    row_used = sorted({i for i, _ in blocks})
    col_used = sorted({j for _, j in blocks})
    depth = min(4, len(blocks))
    reach = len(up)
    any_spec = pl.BlockSpec(memory_space=ANY)
    smem = pl.BlockSpec(memory_space=pltpu.SMEM)
    table = jnp.array([v for i, j in blocks for v in (i, j, row_used.index(i), col_used.index(j))], jnp.int32)
    operands = [area, spot, place, table, front, arrived, arrived_late, *up, *down]
    for j in col_used:
        operands.extend(right[j])
    aliased = so_far is not None
    aliases = {}
    if aliased:
        aliases = {len(operands): 0}
        operands.append(so_far)
    return pl.pallas_call(
        functools.partial(
            update_kernel,
            blocks=tuple(blocks),
            orders=orders,
            per_col=per_col,
            sub_count=sub_count,
            depth=depth,
            reach=reach,
            aliased=aliased,
        ),
        in_specs=[smem] * 4 + [any_spec] * (len(operands) - 4),
        out_specs=[any_spec, pl.BlockSpec(memory_space=pltpu.VMEM)],
        out_shape=[jax.ShapeDtypeStruct(front.shape, jnp.float32), jax.ShapeDtypeStruct((8, 128), jnp.int32)],
        scratch_shapes=[
            pltpu.VMEM((depth, width, part, t, t), jnp.float32),
            pltpu.VMEM((len(row_used), part, t, inner), jnp.bfloat16),
            pltpu.VMEM((len(col_used), width, t, inner), jnp.bfloat16),
            pltpu.VMEM(area.shape + (t, t), arrived.dtype),
            pltpu.SMEM(area.shape, jnp.int32),
            pltpu.SMEM((len(blocks),), jnp.int32),
            pltpu.SMEM(area.shape, jnp.int32),
            pltpu.SMEM((count * count + 1,), jnp.int32),
            pltpu.SemaphoreType.DMA((depth,)),
            pltpu.SemaphoreType.DMA((depth,)),
            pltpu.SemaphoreType.DMA,
            pltpu.SemaphoreType.DMA,
            pltpu.SemaphoreType.DMA,
        ],
        input_output_aliases=aliases,
        compiler_params=params(),
        cost_estimate=pl.CostEstimate(
            flops=2 * len(blocks) * part * t * width * t * inner,
            bytes_accessed=2 * len(blocks) * part * t * width * t * 4,
            transcendentals=0,
        ),
        name="update_blocks",
    )(*operands)


def tie(*values):
    return lax.optimization_barrier(values)


def nearest_first(c, count):
    return sorted(range(count), key=lambda k: (abs(k - c), k))


def exchange(own, late, update_with, so_far, indices, counts):
    _, row_index, col_index = indices
    sub_count, row_count, col_count = counts
    half = own.shape[0] // 2
    spread = row_count == 4 and col_count == 4 and half > 0
    role = row_index ^ col_index
    orders = [nearest_first(c, col_count) for c in range(col_count)]
    up, down, right = [own], [own], []
    done = set()

    def along(value, step, first, last):
        pairs = [(c, c + step) for c in range(first, last) if 0 <= c + step < col_count]
        return lax.ppermute(value, "col", pairs)

    def hop(value, moves):
        pairs = []
        for c in range(col_count):
            for a, b in moves:
                pairs.append(((c ^ a) * col_count + c, (c ^ b) * col_count + c))
        return lax.ppermute(value, ("row", "col"), pairs)

    def advance(so_far, value, most):
        ready = [(i, j) for j in range(len(right)) for i in range(min(len(up), col_count)) if (i, j) not in done]
        ready = ready[:most]
        if not ready:
            return so_far, value
        done.update(ready)
        so_far, token = update_with(late, up, down, right, so_far, ready, orders)
        return so_far, value + token[0, 0]

    batch = col_count * (col_count - 2)
    for n in range(col_count):
        source = own
        if n > 0:
            for c in range(col_count):
                k = orders[c][n]
                piece = up[c - k] if k < c else down[k - c]
                source = piece if c == 0 else jnp.where(col_index == c, piece, source)
        lines = []
        if n + 1 < col_count:
            lines = [along(up[n], 1, n, col_count), along(down[n], -1, 0, col_count - n)]
        busy = spread and n + 1 == col_count
        known = role
        if spread:
            first, second = source[:half], source[half:]
            first_1, second_1 = tie(hop(first, [(0, 1)]), hop(second, [(0, 2)]))
            if busy:
                so_far, known = advance(so_far, known, batch)
            first_2 = hop(jnp.where(known == 0, first, first_1), [(0, 2), (1, 3)])
            second_2 = hop(jnp.where(known == 0, second, second_1), [(0, 1), (2, 3)])
            if n == 0:
                first_2, second_2, late, *lines = tie(first_2, second_2, late, *lines)
            else:
                first_2, second_2, *lines = tie(first_2, second_2, *lines)
            if busy:
                so_far, known = advance(so_far, known, batch)
            whole = jnp.concatenate(
                [
                    jnp.where(known == 0, first, jnp.where(known == 1, first_1, first_2)),
                    jnp.where(known == 0, second, jnp.where(known == 2, second_1, second_2)),
                ],
                0,
            )
        else:
            whole = lax.psum(jnp.where(row_index == col_index, source, jnp.zeros_like(source)), "row")
        if lines:
            up.append(lines[0])
            down.append(lines[1])
        right.append(
            [whole]
            + [lax.ppermute(whole, "sub", [(s, (s + i) % sub_count) for s in range(sub_count)]) for i in range(1, sub_count)]
        )
    while len(done) < col_count * col_count:
        so_far, _ = advance(so_far, role, col_count * col_count)
    return so_far, up + down[1:]


def panel_columns(pieces, col_index, col_count, per_col):
    part, t, width = pieces[0].shape
    mine = []
    for piece in pieces:
        columns = [
            lax.dynamic_slice(piece, (0, 0, (s * col_count + col_index) * t), (part, t, t)) for s in range(per_col)
        ]
        mine.append(jnp.stack(columns, 2))
    ordered = []
    for k in range(col_count):
        rows = mine[0]
        for c in range(col_count):
            if c != k:
                rows = jnp.where(col_index == c, mine[c - k] if k < c else mine[col_count - 1 + k - c], rows)
        ordered.append(rows)
    return jnp.concatenate(ordered, 0)


def local(front, child_tiles, tile_owner, tile_slot):
    row_tiles, _, t, col_tiles, _, _ = front.shape
    sub_count = lax.axis_size("sub")
    row_count = lax.axis_size("row")
    col_count = lax.axis_size("col")
    dev_count = sub_count * row_count * col_count
    tile_count = child_tiles.shape[0]
    capacity = max(2, 2 * tile_count // dev_count)
    panel_tiles = NB // t
    per_col = panel_tiles // col_count
    part = row_tiles // col_count
    local_front = front.reshape(row_tiles, t, col_tiles, t)
    sub_index = lax.axis_index("sub")
    row_index = lax.axis_index("row")
    col_index = lax.axis_index("col")
    group_id = sub_index * row_count + row_index

    axes = ("sub", "row", "col")
    indices = (sub_index, row_index, col_index)
    counts = (sub_count, row_count, col_count)
    is_leading = group_id < panel_tiles
    orders = jnp.array([nearest_first(c, col_count) for c in range(col_count)], jnp.int32)
    place = jnp.concatenate(
        [
            jnp.stack([col_index, sub_index, is_leading]).astype(jnp.int32),
            lax.dynamic_index_in_dim(orders, col_index, 0, keepdims=False),
        ]
    )
    where = jnp.stack(
        [jnp.logical_and(is_leading, col_index == 0), jnp.minimum(group_id, panel_tiles - 1)]
        + [col_index ^ i for i in range(col_count)]
    ).astype(jnp.int32)

    def trade(value, axis, index, count):
        value = value.reshape((count, value.shape[0] // count) + value.shape[1:])
        blocks = [lax.dynamic_index_in_dim(value, index, 0, keepdims=False)]
        for i in range(1, count):
            block = lax.dynamic_index_in_dim(value, index ^ i, 0, keepdims=False)
            blocks.append(lax.ppermute(block, axis, [(k, k ^ i) for k in range(count)]))
        return blocks

    def swap(value, axis):
        return lax.all_to_all(value, axis, split_axis=0, concat_axis=0, tiled=True)

    corner = take_corner(local_front, per_col)
    corner, child_tiles = tie(corner, child_tiles)
    corner = lax.all_gather(corner, axes, axis=0)

    cut = capacity // 2
    first, second, targets = pack(
        tile_owner[:, 0], tile_slot, child_tiles, dev_count, cut, capacity - cut, per_col, col_tiles
    )
    targets = jnp.concatenate(
        [targets[:-1].reshape(dev_count, capacity), jnp.broadcast_to(targets[-1], (dev_count, 1))], 1
    )
    targets = swap(targets, axes)
    lost = jnp.sum(targets[:, capacity])
    landing = targets[:, :cut].reshape(-1)
    landing_all = jnp.concatenate([landing, targets[:, cut:capacity].reshape(-1)])
    landing, landing_all, first = tie(landing, landing_all, first)
    arrived = swap(first.reshape(dev_count, cut, t, t), axes).reshape(-1, t, t)
    arrived, second = tie(arrived, second)
    arrived_late = swap(second.reshape(dev_count, capacity - cut, t, t), axes).reshape(-1, t, t)
    panel = assemble_panel(landing, local_front, arrived, per_col)
    corner, panel = tie(corner, panel)
    lower, inverse = factor(corner, panel_tiles, per_col, col_count)

    width = part * sub_count
    row, column = landing_all // col_tiles, landing_all % col_tiles
    area = jnp.where(landing_all < 0, col_count * col_count, (row // part) * col_count + column // width)
    spot = (row % part) * width + column % width

    def update_with(late, up, down, right, so_far, blocks, orders):
        return update(
            area, spot, place, local_front, arrived, late, up, down, right, so_far, blocks, orders, per_col
        )

    def finish(panel, so_far):
        pieces = trade(panel, "col", col_index, col_count)
        solved = solve(where, pieces, inverse, lower).reshape(part, t, NB)
        updated, rows = exchange(solved, arrived_late, update_with, so_far, indices, counts)
        return updated, panel_columns(rows, col_index, col_count, per_col)

    updated, columns = finish(panel, None)

    def again(state):
        _, before, _ = state
        panel = assemble_panel(landing_all, local_front, jnp.concatenate([arrived, arrived_late]), per_col)
        return (jnp.int32(0),) + finish(panel, before)

    _, updated, columns = lax.while_loop(lambda state: state[0] > 0, again, (lost, updated, columns))
    return (updated.reshape(front.shape), columns.reshape(row_tiles, 1, t, per_col, 1, t))


def solution(mesh):
    return jax.shard_map(
        local,
        mesh=mesh,
        in_specs=(
            P(None, ("sub", "row"), None, None, "col", None),
            P(("sub", "row", "col"), None, None),
            P(("sub", "row", "col"), None),
            P(("sub", "row", "col")),
        ),
        out_specs=(
            P(None, ("sub", "row"), None, None, "col", None),
            P(None, ("sub", "row"), None, None, "col", None),
        ),
        check_vma=False,
    )
```

```python
import functools

import jax
import jax.numpy as jnp
from jax import lax
from jax.experimental import pallas as pl
from jax.experimental.pallas import tpu as pltpu
from jax.sharding import PartitionSpec as P

NB = 1024
ANY = pl.ANY
EXACT = lax.Precision.HIGHEST
VMEM_LIMIT = 56 * 1024 * 1024


def params():
    return pltpu.CompilerParams(vmem_limit_bytes=VMEM_LIMIT)


def contract(a, b, dim_a, dim_b):
    return lax.dot_general(
        a, b, (((dim_a,), (dim_b,)), ((), ())), precision=EXACT, preferred_element_type=jnp.float32
    )


def pack_kernel(owner, slot, tiles, first, second, targets, counts, held, in_sem, sem, *, cut, per_col, col_tiles):
    tile_count = tiles.shape[0]
    dev_count = counts.shape[0]
    late = second.shape[0] // dev_count
    load = pltpu.make_async_copy(tiles, held, in_sem)
    load.start()

    def clear(d, _):
        counts[d] = 0
        for r in range(cut + late):
            targets[d * (cut + late) + r] = -1
        return 0

    lax.fori_loop(0, dev_count, clear, 0)
    load.wait()

    def send(k, lost, panel):
        chosen = lax.rem(slot[k], col_tiles) < per_col
        chosen = chosen if panel else jnp.logical_not(chosen)
        d = owner[k]
        rank = counts[d]

        @pl.when(chosen)
        def _():
            counts[d] = rank + 1
            targets[d * (cut + late) + rank] = slot[k]

            @pl.when(rank < cut)
            def _():
                pltpu.make_async_copy(held.at[k], first.at[d * cut + rank], sem).start()

            @pl.when(rank >= cut)
            def _():
                pltpu.make_async_copy(held.at[k], second.at[d * late + rank - cut], sem).start()

        return lost + jnp.logical_and(chosen, rank >= cut).astype(jnp.int32)

    targets[dev_count * (cut + late)] = lax.fori_loop(0, tile_count, functools.partial(send, panel=True), 0)
    lax.fori_loop(0, tile_count, functools.partial(send, panel=False), 0)
    pltpu.make_async_copy(held, held, sem).wait()


def pack(owner, slot, tiles, dev_count, cut, late, per_col, col_tiles):
    smem = pl.BlockSpec(memory_space=pltpu.SMEM)
    any_spec = pl.BlockSpec(memory_space=ANY)
    return pl.pallas_call(
        functools.partial(pack_kernel, cut=cut, per_col=per_col, col_tiles=col_tiles),
        in_specs=[smem, smem, any_spec],
        out_specs=[any_spec, any_spec, smem],
        out_shape=[
            jax.ShapeDtypeStruct((dev_count * cut,) + tiles.shape[1:], tiles.dtype),
            jax.ShapeDtypeStruct((dev_count * late,) + tiles.shape[1:], tiles.dtype),
            jax.ShapeDtypeStruct((dev_count * (cut + late) + 1,), jnp.int32),
        ],
        scratch_shapes=[
            pltpu.SMEM((dev_count,), jnp.int32),
            pltpu.VMEM(tiles.shape, tiles.dtype),
            pltpu.SemaphoreType.DMA,
            pltpu.SemaphoreType.DMA,
        ],
        compiler_params=params(),
        cost_estimate=pl.CostEstimate(flops=0, bytes_accessed=20_000_000, transcendentals=0),
        name="pack_children",
    )(owner, slot, tiles)


def eliminate(tile):
    n = tile.shape[0]
    groups = n // 8
    rows = lax.broadcasted_iota(jnp.int32, (8, n), 0)
    lanes = lax.broadcasted_iota(jnp.int32, (8, n), 1)
    upper = [tile[8 * h : 8 * h + 8, :] for h in range(groups)]
    ops = [jnp.where(lanes == rows + 8 * h, 1.0, 0.0).astype(jnp.float32) for h in range(groups)]
    column = [jnp.broadcast_to(upper[h][:, 0:1], (8, n)) for h in range(groups)]
    for j in range(n):
        g, u = divmod(j, 8)
        inverse = 1.0 / column[g][u : u + 1, :]
        row = upper[g][u : u + 1, :] * inverse
        row_ops = ops[g][u : u + 1, :] * inverse
        ahead = [None] * groups
        if j + 1 < n:
            g1, u1 = divmod(j + 1, 8)
            scale = column[g1][u1 : u1 + 1, :] * inverse
            for h in range(g1, groups):
                ahead[h] = jnp.broadcast_to(upper[h][:, j + 1 : j + 2], (8, n)) - column[h] * scale
        for h in range(g, groups):
            below = column[h]
            if h == g:
                below = jnp.where(rows > u, below, 0.0)
            upper[h] = upper[h] - below * row
            ops[h] = ops[h] - below * row_ops
        column = ahead
    return jnp.concatenate(upper, 0), jnp.concatenate(ops, 0)


def factor_kernel(corner, lower, inverse, work, copied, sem, *, tiles, per_col, col_count):
    t = corner.shape[-1]
    rows = lax.broadcasted_iota(jnp.int32, (t, t), 0)
    cols = lax.broadcasted_iota(jnp.int32, (t, t), 1)
    copies = []
    for p in range(tiles):
        for j in range(p + 1):
            copies.append(
                pltpu.make_async_copy(
                    corner.at[p * col_count + j % col_count, j // col_count], copied.at[p, j], sem
                )
            )
    for copy in copies:
        copy.start()
    lower[...] = jnp.zeros_like(lower)
    for copy in copies:
        copy.wait()

    for p in range(tiles):
        for j in range(p + 1):
            block = copied[p, j]
            if p == j:
                block = jnp.where(rows >= cols, block, block.T)
                work[p, :, p * t : (p + 1) * t] = block
            else:
                work[p, :, j * t : (j + 1) * t] = block
                work[j, :, p * t : (p + 1) * t] = block.T

    def step(j, _):
        here = pl.ds(pl.multiple_of(j * t, t), t)
        upper, ops = eliminate(work[j, :, here])
        pivots = jnp.sum(jnp.where(rows == cols, upper, 0.0), 1, keepdims=True)
        scale = lax.rsqrt(pivots)
        upper = jnp.where(rows <= cols, upper * scale, 0.0)
        ops = jnp.where(rows >= cols, ops * scale, 0.0)
        lower[pl.ds(pl.multiple_of(j * t, t), t), here] = upper.T.astype(lower.dtype)
        work[j, :, here] = jnp.where(rows == cols, 1.0, 0.0)
        work[j] = contract(ops, work[j], 1, 0)

        def below(i, _):
            block = contract(work[i, :, here], ops, 1, 1)
            lower[pl.ds(pl.multiple_of(i * t, t), t), here] = block.astype(lower.dtype)
            work[i, :, here] = jnp.zeros((t, t), jnp.float32)
            work[i] = work[i] - contract(block, work[j], 1, 0)
            return 0

        lax.fori_loop(j + 1, tiles, below, 0)
        return 0

    lax.fori_loop(0, tiles, step, 0)
    wide_rows = lax.broadcasted_iota(jnp.int32, (t, tiles * t), 1)
    for p in range(tiles):
        inverse[p * t : (p + 1) * t, :] = jnp.where(wide_rows < (p + 1) * t, work[p], 0.0)


def factor(corner, tiles, per_col, col_count):
    t = corner.shape[-1]
    n = tiles * t
    vmem = pl.BlockSpec(memory_space=pltpu.VMEM)
    return pl.pallas_call(
        functools.partial(factor_kernel, tiles=tiles, per_col=per_col, col_count=col_count),
        in_specs=[pl.BlockSpec(memory_space=ANY)],
        out_specs=[vmem, vmem],
        out_shape=[jax.ShapeDtypeStruct((n, n), jnp.bfloat16), jax.ShapeDtypeStruct((n, n), jnp.float32)],
        scratch_shapes=[
            pltpu.VMEM((tiles, t, n), jnp.float32),
            pltpu.VMEM((tiles, tiles, t, t), jnp.float32),
            pltpu.SemaphoreType.DMA,
        ],
        compiler_params=params(),
        cost_estimate=pl.CostEstimate(flops=100_000_000_000, bytes_accessed=200_000_000, transcendentals=0),
        name="factor_corner",
    )(corner)


def corner_kernel(front, out, held, in_sem, out_sem):
    per_col = out.shape[0]
    copies = [pltpu.make_async_copy(front.at[0, :, s, :], held.at[s], in_sem.at[s]) for s in range(per_col)]
    for copy in copies:
        copy.start()
    for copy in copies:
        copy.wait()
    copy = pltpu.make_async_copy(held, out, out_sem)
    copy.start()
    copy.wait()


def take_corner(front, per_col):
    _, t, _, _ = front.shape
    any_spec = pl.BlockSpec(memory_space=ANY)
    return pl.pallas_call(
        corner_kernel,
        in_specs=[any_spec],
        out_specs=any_spec,
        out_shape=jax.ShapeDtypeStruct((per_col, t, t), front.dtype),
        scratch_shapes=[
            pltpu.VMEM((per_col, t, t), front.dtype),
            pltpu.SemaphoreType.DMA((per_col,)),
            pltpu.SemaphoreType.DMA,
        ],
        compiler_params=params(),
        cost_estimate=pl.CostEstimate(flops=0, bytes_accessed=500_000, transcendentals=0),
        name="take_corner",
    )(front)


def panel_kernel(landing, front, arrived, out, buf, tiles, picked, in_sem, tile_sem, out_sem, *, per_col, col_tiles):
    slots = landing.shape[0]

    def front_copy(s):
        return pltpu.make_async_copy(front.at[:, :, s, :], buf.at[:, s], in_sem)

    for s in range(per_col):
        front_copy(s).start()

    def find(k, n):
        slot = landing[k]
        hit = jnp.logical_and(slot >= 0, lax.rem(slot, col_tiles) < per_col)

        @pl.when(hit)
        def _():
            picked[n] = slot
            pltpu.make_async_copy(arrived.at[k], tiles.at[n], tile_sem).start()

        return n + hit.astype(jnp.int32)

    found = lax.fori_loop(0, slots, find, 0)
    for s in range(per_col):
        front_copy(s).wait()

    def wait(n, _):
        pltpu.make_async_copy(arrived.at[0], tiles.at[0], tile_sem).wait()
        return 0

    lax.fori_loop(0, found, wait, 0)

    def add(n, _):
        q = picked[n] // col_tiles
        s = lax.rem(picked[n], col_tiles)
        buf[q, s] = buf[q, s] + tiles[n].astype(jnp.float32)
        return 0

    lax.fori_loop(0, found, add, 0)
    copy = pltpu.make_async_copy(buf, out, out_sem)
    copy.start()
    copy.wait()


def assemble_panel(landing, front, arrived, per_col):
    row_tiles, t, col_tiles, _ = front.shape
    any_spec = pl.BlockSpec(memory_space=ANY)
    return pl.pallas_call(
        functools.partial(panel_kernel, per_col=per_col, col_tiles=col_tiles),
        in_specs=[pl.BlockSpec(memory_space=pltpu.SMEM), any_spec, any_spec],
        out_specs=any_spec,
        out_shape=jax.ShapeDtypeStruct((row_tiles, per_col, t, t), jnp.float32),
        scratch_shapes=[
            pltpu.VMEM((row_tiles, per_col, t, t), jnp.float32),
            pltpu.VMEM(arrived.shape, arrived.dtype),
            pltpu.SMEM(landing.shape, jnp.int32),
            pltpu.SemaphoreType.DMA,
            pltpu.SemaphoreType.DMA,
            pltpu.SemaphoreType.DMA,
        ],
        compiler_params=params(),
        cost_estimate=pl.CostEstimate(flops=0, bytes_accessed=20_000_000, transcendentals=0),
        name="assemble_panel",
    )(landing, front, arrived)


def solve_kernel(where, inverse, lower, *rest, col_count):
    pieces, rest = rest[:col_count], rest[col_count:]
    solved, rows, inverse_v, lead, sem, inv_sem, lead_sem = rest
    part, per_col, t, _ = pieces[0].shape
    for i in range(col_count):
        origin = where[2 + i]
        for q in range(part):
            for s in range(per_col):
                column = pl.multiple_of((s * col_count + origin) * t, t)
                pltpu.make_async_copy(
                    pieces[i].at[q, s], rows.at[pl.ds(q * t, t), pl.ds(column, t)], sem
                ).start()
    inv_copy = pltpu.make_async_copy(inverse, inverse_v, inv_sem)
    inv_copy.start()
    lead_copy = pltpu.make_async_copy(lower.at[pl.ds(where[1] * t, t)], lead, lead_sem)
    lead_copy.start()
    pltpu.make_async_copy(rows, rows, sem).wait()
    inv_copy.wait()
    lead_copy.wait()
    n = inverse.shape[0]
    step = 2 * t if n % (2 * t) == 0 else t
    for b in range(0, n, step):
        product = contract(rows[:, : b + step], inverse_v[b : b + step, : b + step], 1, 1)
        solved[:, b : b + step] = product.astype(solved.dtype)

    @pl.when(where[0] == 1)
    def _():
        solved[:t, :] = lead[...]


def solve(where, pieces, inverse, lower):
    part, _, t, _ = pieces[0].shape
    n = inverse.shape[0]
    any_spec = pl.BlockSpec(memory_space=ANY)
    return pl.pallas_call(
        functools.partial(solve_kernel, col_count=len(pieces)),
        in_specs=[pl.BlockSpec(memory_space=pltpu.SMEM)] + [any_spec] * (2 + len(pieces)),
        out_specs=pl.BlockSpec(memory_space=pltpu.VMEM),
        out_shape=jax.ShapeDtypeStruct((part * t, n), jnp.bfloat16),
        scratch_shapes=[
            pltpu.VMEM((part * t, n), jnp.float32),
            pltpu.VMEM((n, n), jnp.float32),
            pltpu.VMEM((t, n), jnp.bfloat16),
            pltpu.SemaphoreType.DMA,
            pltpu.SemaphoreType.DMA,
            pltpu.SemaphoreType.DMA,
        ],
        compiler_params=params(),
        cost_estimate=pl.CostEstimate(flops=8_000_000_000, bytes_accessed=12_000_000, transcendentals=0),
        name="solve_rows",
    )(where, inverse, lower, *pieces)


def update_kernel(
    area, spot, place, table, front, arrived, arrived_late, *rest,
    blocks, orders, per_col, sub_count, depth, reach, aliased,
):
    row_used = sorted({i for i, _ in blocks})
    col_used = sorted({j for _, j in blocks})
    ups, rest = rest[:reach], rest[reach:]
    downs, rest = rest[:reach], rest[reach:]
    right, rest = rest[: len(col_used) * sub_count], rest[len(col_used) * sub_count :]
    rest = rest[1:] if aliased else rest
    out, token, buf, left_v, right_v, tiles, picked, head, following, lookup = rest[:10]
    in_sem, out_sem, left_sem, right_sem, tile_sem = rest[10:]
    token[...] = jnp.zeros_like(token)
    early = arrived.shape[0]
    t = front.shape[1]
    slots = area.shape[0]
    steps = len(blocks)
    part = ups[0].shape[0]
    count = len(orders)
    width = part * sub_count

    def corner_of(b):
        return place[3 + table[4 * b]], place[3 + table[4 * b + 1]]

    def read(b, slot):
        rows, cols = corner_of(b)
        for j in range(width):
            source = front.at[pl.ds(rows * part, part), :, cols * width + j, :]
            pltpu.make_async_copy(source, buf.at[slot, j], in_sem.at[slot]).start()

    def write(b, slot):
        rows, cols = corner_of(b)
        for j in range(width):
            target = out.at[pl.ds(rows * part, part), :, cols * width + j, :]
            pltpu.make_async_copy(buf.at[slot, j], target, out_sem.at[slot]).start()

    def drain(slot, sem):
        pltpu.make_async_copy(buf.at[slot], buf.at[slot], sem.at[slot]).wait()

    for n, i in enumerate(row_used):
        for c in range(count):
            k = orders[c][i]

            @pl.when(place[0] == c)
            def _(n=n, c=c, k=k):
                piece = ups[c - k] if k <= c else downs[k - c]
                pltpu.make_async_copy(piece, left_v.at[n], left_sem).start()

    for n in range(len(col_used)):
        for i in range(sub_count):
            origin = lax.rem(place[1] + sub_count - i, sub_count)
            for r in range(part):
                pltpu.make_async_copy(
                    right[n * sub_count + i].at[r], right_v.at[n, r * sub_count + origin], right_sem
                ).start()
    ahead = depth - 2
    for b in range(min(ahead, steps)):
        read(b, b)

    for k in range(count * count + 1):
        lookup[k] = -1
    for b in range(steps):
        head[b] = -1
        rows, cols = corner_of(b)
        lookup[rows * count + cols] = b

    def find(k, n):
        b = lookup[area[k]]
        hit = b >= 0

        @pl.when(hit)
        def _():
            picked[n] = spot[k]
            following[n] = head[b]
            head[b] = n

            @pl.when(k < early)
            def _():
                pltpu.make_async_copy(arrived.at[k], tiles.at[n], tile_sem).start()

            @pl.when(k >= early)
            def _():
                pltpu.make_async_copy(arrived_late.at[k - early], tiles.at[n], tile_sem).start()

        return n + hit.astype(jnp.int32)

    found = lax.fori_loop(0, slots, find, 0)
    pltpu.make_async_copy(left_v, left_v, left_sem).wait()
    for n, i in enumerate(row_used):

        @pl.when(jnp.logical_and(place[2] == 1, place[3 + i] == 0))
        def _(n=n):
            left_v[n, 0] = jnp.zeros_like(left_v[n, 0])

    pltpu.make_async_copy(right_v, right_v, right_sem).wait()
    for n, j in enumerate(col_used):

        @pl.when(place[3 + j] == 0)
        def _(n=n):
            right_v[n, :per_col] = jnp.zeros_like(right_v[n, :per_col])

    def wait_tile(n, _):
        pltpu.make_async_copy(arrived.at[0], tiles.at[0], tile_sem).wait()
        return 0

    lax.fori_loop(0, found, wait_tile, 0)

    def step(b, _):
        slot = lax.rem(b, depth)

        @pl.when(b + ahead < steps)
        def _():
            later = lax.rem(b + ahead, depth)

            @pl.when(b + ahead >= depth)
            def _():
                drain(later, out_sem)

            read(b + ahead, later)

        drain(slot, in_sem)
        rows = left_v[table[4 * b + 2]].reshape(part * t, left_v.shape[-1])
        cols = right_v[table[4 * b + 3]].reshape(width * t, right_v.shape[-1])
        product = lax.dot_general(rows, cols, (((1,), (1,)), ((), ())), preferred_element_type=jnp.float32)
        for j in range(width):
            piece = product[:, j * t : (j + 1) * t].reshape(part, t, t)
            buf[slot, j] = buf[slot, j] - piece

        def add(n):
            j, q = lax.rem(picked[n], width), lax.div(picked[n], width)
            buf[slot, j, q] = buf[slot, j, q] + tiles[n].astype(jnp.float32)
            return following[n]

        lax.while_loop(lambda n: n >= 0, add, head[b])
        write(b, slot)
        return 0

    lax.fori_loop(0, steps, step, 0)
    for b in range(max(0, steps - depth), steps):
        drain(b % depth, out_sem)


def update(area, spot, place, front, arrived, arrived_late, up, down, right, so_far, blocks, orders, per_col):
    t = front.shape[1]
    sub_count = len(right[0])
    part, _, inner = up[0].shape
    width = part * sub_count
    count = len(orders)
    row_used = sorted({i for i, _ in blocks})
    col_used = sorted({j for _, j in blocks})
    depth = max(3, min(5, len(blocks) + 1))
    reach = len(up)
    any_spec = pl.BlockSpec(memory_space=ANY)
    smem = pl.BlockSpec(memory_space=pltpu.SMEM)
    table = jnp.array([v for i, j in blocks for v in (i, j, row_used.index(i), col_used.index(j))], jnp.int32)
    operands = [area, spot, place, table, front, arrived, arrived_late, *up, *down]
    for j in col_used:
        operands.extend(right[j])
    aliased = so_far is not None
    aliases = {}
    if aliased:
        aliases = {len(operands): 0}
        operands.append(so_far)
    return pl.pallas_call(
        functools.partial(
            update_kernel,
            blocks=tuple(blocks),
            orders=orders,
            per_col=per_col,
            sub_count=sub_count,
            depth=depth,
            reach=reach,
            aliased=aliased,
        ),
        in_specs=[smem] * 4 + [any_spec] * (len(operands) - 4),
        out_specs=[any_spec, pl.BlockSpec(memory_space=pltpu.VMEM)],
        out_shape=[jax.ShapeDtypeStruct(front.shape, jnp.float32), jax.ShapeDtypeStruct((8, 128), jnp.int32)],
        scratch_shapes=[
            pltpu.VMEM((depth, width, part, t, t), jnp.float32),
            pltpu.VMEM((len(row_used), part, t, inner), jnp.bfloat16),
            pltpu.VMEM((len(col_used), width, t, inner), jnp.bfloat16),
            pltpu.VMEM(area.shape + (t, t), arrived.dtype),
            pltpu.SMEM(area.shape, jnp.int32),
            pltpu.SMEM((len(blocks),), jnp.int32),
            pltpu.SMEM(area.shape, jnp.int32),
            pltpu.SMEM((count * count + 1,), jnp.int32),
            pltpu.SemaphoreType.DMA((depth,)),
            pltpu.SemaphoreType.DMA((depth,)),
            pltpu.SemaphoreType.DMA,
            pltpu.SemaphoreType.DMA,
            pltpu.SemaphoreType.DMA,
        ],
        input_output_aliases=aliases,
        compiler_params=params(),
        cost_estimate=pl.CostEstimate(
            flops=2 * len(blocks) * part * t * width * t * inner,
            bytes_accessed=2 * len(blocks) * part * t * width * t * 4,
            transcendentals=0,
        ),
        name="update_blocks",
    )(*operands)


def tie(*values):
    return lax.optimization_barrier(values)


def nearest_first(c, count):
    return sorted(range(count), key=lambda k: (abs(k - c), k))


def exchange(own, late, update_with, so_far, indices, counts):
    _, row_index, col_index = indices
    sub_count, row_count, col_count = counts
    half = own.shape[0] // 2
    spread = row_count == 4 and col_count == 4 and half > 0
    role = row_index ^ col_index
    orders = [nearest_first(c, col_count) for c in range(col_count)]
    up, down, right = [own], [own], []
    done = set()

    def along(value, step, first, last):
        pairs = [(c, c + step) for c in range(first, last) if 0 <= c + step < col_count]
        return lax.ppermute(value, "col", pairs)

    def hop(value, moves):
        pairs = []
        for c in range(col_count):
            for a, b in moves:
                pairs.append(((c ^ a) * col_count + c, (c ^ b) * col_count + c))
        return lax.ppermute(value, ("row", "col"), pairs)

    def advance(so_far, value, most):
        ready = [(i, j) for j in range(len(right)) for i in range(min(len(up), col_count)) if (i, j) not in done]
        ready = ready[:most]
        if not ready:
            return so_far, value
        done.update(ready)
        so_far, token = update_with(late, up, down, right, so_far, ready, orders)
        return so_far, value + token[0, 0]

    batch = col_count * (col_count - 2)
    for n in range(col_count):
        source = own
        if n > 0:
            for c in range(col_count):
                k = orders[c][n]
                piece = up[c - k] if k < c else down[k - c]
                source = piece if c == 0 else jnp.where(col_index == c, piece, source)
        lines = []
        if n + 1 < col_count:
            lines = [along(up[n], 1, n, col_count), along(down[n], -1, 0, col_count - n)]
        busy = spread and n + 1 == col_count
        known = role
        if spread:
            first, second = source[:half], source[half:]
            first_1, second_1 = tie(hop(first, [(0, 1)]), hop(second, [(0, 2)]))
            if busy:
                so_far, known = advance(so_far, known, batch)
            first_2 = hop(jnp.where(known == 0, first, first_1), [(0, 2), (1, 3)])
            second_2 = hop(jnp.where(known == 0, second, second_1), [(0, 1), (2, 3)])
            if n == 0:
                first_2, second_2, late, *lines = tie(first_2, second_2, late, *lines)
            else:
                first_2, second_2, *lines = tie(first_2, second_2, *lines)
            if busy:
                so_far, known = advance(so_far, known, batch)
            whole = jnp.concatenate(
                [
                    jnp.where(known == 0, first, jnp.where(known == 1, first_1, first_2)),
                    jnp.where(known == 0, second, jnp.where(known == 2, second_1, second_2)),
                ],
                0,
            )
        else:
            whole = lax.psum(jnp.where(row_index == col_index, source, jnp.zeros_like(source)), "row")
        if lines:
            up.append(lines[0])
            down.append(lines[1])
        right.append(
            [whole]
            + [lax.ppermute(whole, "sub", [(s, (s + i) % sub_count) for s in range(sub_count)]) for i in range(1, sub_count)]
        )
    while len(done) < col_count * col_count:
        so_far, _ = advance(so_far, role, col_count * col_count)
    return so_far, up + down[1:]


def panel_columns(pieces, col_index, col_count, per_col):
    part, t, width = pieces[0].shape
    mine = []
    for piece in pieces:
        columns = [
            lax.dynamic_slice(piece, (0, 0, (s * col_count + col_index) * t), (part, t, t)) for s in range(per_col)
        ]
        mine.append(jnp.stack(columns, 2))
    ordered = []
    for k in range(col_count):
        rows = mine[0]
        for c in range(col_count):
            if c != k:
                rows = jnp.where(col_index == c, mine[c - k] if k < c else mine[col_count - 1 + k - c], rows)
        ordered.append(rows)
    return jnp.concatenate(ordered, 0)


def local(front, child_tiles, tile_owner, tile_slot):
    row_tiles, _, t, col_tiles, _, _ = front.shape
    sub_count = lax.axis_size("sub")
    row_count = lax.axis_size("row")
    col_count = lax.axis_size("col")
    dev_count = sub_count * row_count * col_count
    tile_count = child_tiles.shape[0]
    capacity = max(2, 2 * tile_count // dev_count)
    panel_tiles = NB // t
    per_col = panel_tiles // col_count
    part = row_tiles // col_count
    local_front = front.reshape(row_tiles, t, col_tiles, t)
    sub_index = lax.axis_index("sub")
    row_index = lax.axis_index("row")
    col_index = lax.axis_index("col")
    group_id = sub_index * row_count + row_index

    axes = ("sub", "row", "col")
    indices = (sub_index, row_index, col_index)
    counts = (sub_count, row_count, col_count)
    is_leading = group_id < panel_tiles
    orders = jnp.array([nearest_first(c, col_count) for c in range(col_count)], jnp.int32)
    place = jnp.concatenate(
        [
            jnp.stack([col_index, sub_index, is_leading]).astype(jnp.int32),
            lax.dynamic_index_in_dim(orders, col_index, 0, keepdims=False),
        ]
    )
    where = jnp.stack(
        [jnp.logical_and(is_leading, col_index == 0), jnp.minimum(group_id, panel_tiles - 1)]
        + [col_index ^ i for i in range(col_count)]
    ).astype(jnp.int32)

    def trade(value, axis, index, count):
        value = value.reshape((count, value.shape[0] // count) + value.shape[1:])
        blocks = [lax.dynamic_index_in_dim(value, index, 0, keepdims=False)]
        for i in range(1, count):
            block = lax.dynamic_index_in_dim(value, index ^ i, 0, keepdims=False)
            blocks.append(lax.ppermute(block, axis, [(k, k ^ i) for k in range(count)]))
        return blocks

    def swap(value, axis):
        return lax.all_to_all(value, axis, split_axis=0, concat_axis=0, tiled=True)

    corner = take_corner(local_front, per_col)
    corner, child_tiles = tie(corner, child_tiles)
    corner = lax.all_gather(corner, axes, axis=0)

    cut = capacity // 2
    first, second, targets = pack(
        tile_owner[:, 0], tile_slot, child_tiles, dev_count, cut, capacity - cut, per_col, col_tiles
    )
    targets = jnp.concatenate(
        [targets[:-1].reshape(dev_count, capacity), jnp.broadcast_to(targets[-1], (dev_count, 1))], 1
    )
    targets = swap(targets, axes)
    lost = jnp.sum(targets[:, capacity])
    landing = targets[:, :cut].reshape(-1)
    landing_all = jnp.concatenate([landing, targets[:, cut:capacity].reshape(-1)])
    landing, landing_all, first = tie(landing, landing_all, first)
    arrived = swap(first.reshape(dev_count, cut, t, t), axes).reshape(-1, t, t)
    arrived, second = tie(arrived, second)
    arrived_late = swap(second.reshape(dev_count, capacity - cut, t, t), axes).reshape(-1, t, t)
    panel = assemble_panel(landing, local_front, arrived, per_col)
    corner, panel = tie(corner, panel)
    lower, inverse = factor(corner, panel_tiles, per_col, col_count)

    width = part * sub_count
    row, column = landing_all // col_tiles, landing_all % col_tiles
    area = jnp.where(landing_all < 0, col_count * col_count, (row // part) * col_count + column // width)
    spot = (row % part) * width + column % width

    def update_with(late, up, down, right, so_far, blocks, orders):
        return update(
            area, spot, place, local_front, arrived, late, up, down, right, so_far, blocks, orders, per_col
        )

    def finish(panel, so_far):
        pieces = trade(panel, "col", col_index, col_count)
        solved = solve(where, pieces, inverse, lower).reshape(part, t, NB)
        updated, rows = exchange(solved, arrived_late, update_with, so_far, indices, counts)
        return updated, panel_columns(rows, col_index, col_count, per_col)

    updated, columns = finish(panel, None)

    def again(state):
        _, before, _ = state
        panel = assemble_panel(landing_all, local_front, jnp.concatenate([arrived, arrived_late]), per_col)
        return (jnp.int32(0),) + finish(panel, before)

    _, updated, columns = lax.while_loop(lambda state: state[0] > 0, again, (lost, updated, columns))
    return (updated.reshape(front.shape), columns.reshape(row_tiles, 1, t, per_col, 1, t))


def solution(mesh):
    return jax.shard_map(
        local,
        mesh=mesh,
        in_specs=(
            P(None, ("sub", "row"), None, None, "col", None),
            P(("sub", "row", "col"), None, None),
            P(("sub", "row", "col"), None),
            P(("sub", "row", "col")),
        ),
        out_specs=(
            P(None, ("sub", "row"), None, None, "col", None),
            P(None, ("sub", "row"), None, None, "col", None),
        ),
        check_vma=False,
    )
```
